32 devices in a mesh: grp: 2 (over y), seq: 4 (over z), blk: 4 (over x, core).
Axes of the slice: x: 2, y: 2, z: 4, core: 2. Of those that a mesh axis runs over, the one named last changes fastest.
Arguments:
- queries: bfloat16 [2048, 64, 128], P(('grp', 'seq', 'blk')), parts along dimension 0, may hold values from -6 to 6
- keys: bfloat16 [2048, 8, 128], P(('grp', 'seq', 'blk')), parts along dimension 0, may hold values from -6 to 6
- values: bfloat16 [2048, 8, 128], P(('grp', 'seq', 'blk')), parts along dimension 0, may hold values from -6 to 6
- vert_blocks: int32 [64, 16], replicated, may hold values from 0 to 15, as said below
- vert_count: int32 [64], replicated, may hold values from 1 to 16, as said below
- slash_offsets: int32 [64, 14], replicated, may hold values from 0 to 15, as said below
- slash_count: int32 [64], replicated, may hold values from 1 to 14, as said below
Outputs:
- attended: bfloat16 [2048, 64, 128], P(('grp', 'seq', 'blk')), parts along dimension 0
The draws below stay inside these ranges and needn't reach their ends.
There are 2 independent parts, one for each index of `grp`. The reference program is written for one: setup_inputs(seed, part) draws one part's arguments, and reference() takes and returns one part's arrays. A program takes and returns all parts, laid end to end along the dimension named above; an argument that names none is the same for every part. Nothing has to cross between parts.
Inputs may be any that keep to these rules, and one draw needn't show every extreme that they name: `vert_blocks`: the 16 entries of each head's row are distinct. `vert_count`: some head uses all 16 entries. `slash_offsets`: the 14 entries of each head's row are distinct, and the first is 0. `slash_count`: some head uses all 14 entries.
All inputs are finite; a program needn't handle non-finite values.
Results may differ from the reference program's by a relative error of at most 0.0047.
Values may be sent and summed in bfloat16 or wider, within the bound.
No kernel may reach another device: no remote copies, remote signals or barrier semaphores. Data moves between devices by JAX's collectives and lax.ppermute only.
A program may use at most 64 MiB of HBM per device.

```python
import math
import jax
import jax.numpy as jnp
from jax import lax

HQ = 64
KVH = 8
HD = 128
BLOCK = 64
NV = 16
NS = 14
SEQ_LEN = 1024
NBLOCKS = 16


def draw_queries(key, part):
    key = jax.random.fold_in(key, 3)
    normal_key = jax.random.fold_in(key, 0)
    result = jax.random.normal(normal_key, (SEQ_LEN, HQ, HD), jnp.float32)
    return jnp.clip(result, -6.0, 6.0).astype(jnp.bfloat16)


def draw_keys(key, part):
    key = jax.random.fold_in(key, 5)
    normal_key = jax.random.fold_in(key, 0)
    result = jax.random.normal(normal_key, (SEQ_LEN, KVH, HD), jnp.float32)
    return jnp.clip(result, -6.0, 6.0).astype(jnp.bfloat16)


def draw_vert_blocks(key, part):
    key = jax.random.fold_in(key, 7)
    head_keys = jax.random.split(key, HQ)

    def one_head(one_key):
        return jax.random.permutation(one_key, NBLOCKS)[:NV].astype(jnp.int32)
    return jax.vmap(one_head)(head_keys)


def draw_vert_count(key, part):
    key = jax.random.fold_in(key, 9)
    count_key, pick_key = jax.random.split(key)
    counts = jax.random.randint(count_key, (HQ,), 1, NV + 1, dtype=jnp.int32)
    chosen = jax.random.randint(pick_key, (), 0, HQ, dtype=jnp.int32)
    return jnp.where(jnp.arange(HQ, dtype=jnp.int32) == chosen, NV, counts).astype(jnp.int32)


def draw_slash_offsets(key, part):
    key = jax.random.fold_in(key, 13)
    head_keys = jax.random.split(key, HQ)

    def one_head(one_key):
        later = jax.random.permutation(one_key, NBLOCKS - 1)[:NS - 1] + 1
        return jnp.concatenate([jnp.zeros((1,), jnp.int32), later.astype(jnp.int32)])
    return jax.vmap(one_head)(head_keys)


def draw_slash_count(key, part):
    key = jax.random.fold_in(key, 17)
    count_key, pick_key = jax.random.split(key)
    counts = jax.random.randint(count_key, (HQ,), 1, NS + 1, dtype=jnp.int32)
    chosen = jax.random.randint(pick_key, (), 0, HQ, dtype=jnp.int32)
    return jnp.where(jnp.arange(HQ, dtype=jnp.int32) == chosen, NS, counts).astype(jnp.int32)


def level_of(own_key, extent, cuts, smallest, high):
    gain = 1.0
    for dim, blocks in cuts:
        draws = jax.random.uniform(jax.random.fold_in(jax.random.fold_in(own_key, 6), dim), (blocks,), jnp.float32, smallest / len(cuts), high / len(cuts))
        gain = gain * jnp.repeat(jnp.exp(draws), extent[dim] // blocks).reshape((-1,) + (1,) * (len(extent) - 1 - dim))
    return gain


def bell_draw(key, dims, scale, bound, cuts=(), held_as=jnp.bfloat16):
    level = level_of(key, dims, cuts, -0.22, 0.18) if cuts else 1.0
    array = jax.random.normal(key, dims, jnp.float32) * scale * level
    return jnp.minimum(jnp.maximum(array, -bound), bound).astype(held_as)


def setup_inputs(seed: int = 0, part: int = 0) -> dict:
    seeds = jax.random.split(jax.random.key(seed), 8)
    part_keys = jax.random.split(jax.random.fold_in(seeds[7], part), 8)
    queries = draw_queries(jax.random.fold_in(jax.random.fold_in(seeds[7], part), 71), part)
    keys = draw_keys(jax.random.fold_in(jax.random.fold_in(seeds[7], part), 71), part)
    values = bell_draw(part_keys[2], (SEQ_LEN, KVH, HD), 1.0, 6.0, ((0, 16),))
    vert_blocks = draw_vert_blocks(jax.random.fold_in(seeds[7], 71), part)
    vert_count = draw_vert_count(jax.random.fold_in(seeds[7], 71), part)
    slash_offsets = draw_slash_offsets(jax.random.fold_in(seeds[7], 71), part)
    slash_count = draw_slash_count(jax.random.fold_in(seeds[7], 71), part)
    return {"queries": queries, "keys": keys, "values": values, "vert_blocks": vert_blocks, "vert_count": vert_count, "slash_offsets": slash_offsets, "slash_count": slash_count}


def slash_plan(query_index, vertical, vert_live, slash, slash_live):
    slash_index = query_index[:, None] - slash[None, :]
    duplicate = jnp.any((slash_index[:, :, None] == vertical[None, None, :]) & vert_live[None, None, :], axis=2)
    usable = slash_live[None, :] & (slash_index >= 0) & jnp.logical_not(duplicate)
    return (slash_index, usable)

def sparse_block(query_tiles, query_index, vert_keys, vert_values, vertical, vert_live, slash_keys, slash_values, slash_index, slash_live):
    tile_count, block_len, head_width = query_tiles.shape
    lane_pos = jnp.arange(block_len, dtype=jnp.int32)
    query_pos = query_index[:, None] * block_len + lane_pos[None, :]
    vert_pos = vertical[:, None] * block_len + lane_pos[None, :]
    slash_pos = slash_index[:, :, None] * block_len + lane_pos[None, None, :]
    score_scale = 1.0 / math.sqrt(head_width)
    query_wide = query_tiles.astype(jnp.float32)
    vert_scores = jnp.einsum('gid,vjd->givj', query_wide, vert_keys.astype(jnp.float32)) * score_scale
    slash_scores = jnp.einsum('gid,gsjd->gisj', query_wide, slash_keys.astype(jnp.float32)) * score_scale
    vert_mask = vert_live[None, None, :, None] & (vert_pos[None, None, :, :] <= query_pos[:, :, None, None])
    slash_mask = slash_live[:, None, :, None] & (slash_pos[:, None, :, :] <= query_pos[:, :, None, None])
    scores = jnp.concatenate([jnp.where(vert_mask, vert_scores, -jnp.inf).reshape(tile_count, block_len, -1), jnp.where(slash_mask, slash_scores, -jnp.inf).reshape(tile_count, block_len, -1)], axis=2)
    row_max = lax.optimization_barrier(jnp.max(scores, axis=2, keepdims=True))
    raised = jnp.exp(scores - row_max)
    weights = (raised / lax.optimization_barrier(jnp.sum(raised, axis=2, keepdims=True))).astype(jnp.bfloat16)
    vert_width = vert_keys.shape[0] * block_len
    result = jnp.einsum('gik,kd->gid', weights[:, :, :vert_width].astype(jnp.float32), vert_values.reshape(vert_width, head_width).astype(jnp.float32))
    result = result + jnp.einsum('gik,gkd->gid', weights[:, :, vert_width:].astype(jnp.float32), slash_values.reshape(tile_count, -1, head_width).astype(jnp.float32))
    return result.astype(jnp.bfloat16).reshape(tile_count * block_len, head_width)

def reference(queries, keys, values, vert_blocks, vert_count, slash_offsets, slash_count):
    block_total = SEQ_LEN // BLOCK
    head_queries = jnp.transpose(queries, (1, 0, 2)).reshape(HQ, block_total, BLOCK, HD)
    key_tiles = jnp.transpose(keys, (1, 0, 2)).reshape(KVH, block_total, BLOCK, HD)
    value_tiles = jnp.transpose(values, (1, 0, 2)).reshape(KVH, block_total, BLOCK, HD)
    query_index = jnp.arange(block_total, dtype=jnp.int32)

    def one_head(head_id):
        kv_group = head_id // (HQ // KVH)
        query_tiles = head_queries[head_id]
        head_keys = key_tiles[kv_group]
        head_values = value_tiles[kv_group]
        vertical = vert_blocks[head_id].astype(jnp.int32)
        vert_live = jnp.arange(NV, dtype=jnp.int32) < vert_count[head_id]
        slash_live = jnp.arange(NS, dtype=jnp.int32) < slash_count[head_id]
        slash_index, usable = slash_plan(query_index, vertical, vert_live, slash_offsets[head_id].astype(jnp.int32), slash_live)
        clamped = jnp.clip(slash_index, 0, block_total - 1).astype(jnp.int32)
        return sparse_block(query_tiles, query_index, head_keys[vertical], head_values[vertical], vertical, vert_live, head_keys[clamped], head_values[clamped], slash_index, usable)
    attended = lax.map(one_head, jnp.arange(HQ, dtype=jnp.int32))
    return jnp.transpose(attended, (1, 0, 2))
```

```python
import functools
import math

import jax
import jax.numpy as jnp
from jax import lax
from jax.experimental import pallas as pl
from jax.experimental.pallas import tpu as pltpu
from jax.sharding import PartitionSpec as P

BLOCK = 64
NEG = -1e30
GATHER_BYTES = 8 << 20


def slash_plan(query_index, vertical, vert_live, slash, slash_live):
    slash_index = query_index[:, None] - slash[None, :]
    duplicate = jnp.any(
        (slash_index[:, :, None] == vertical[None, None, :]) & vert_live[None, None, :], axis=2
    )
    usable = slash_live[None, :] & (slash_index >= 0) & jnp.logical_not(duplicate)
    return (slash_index, usable)


def sparse_block(
    query_tiles,
    query_index,
    vert_keys,
    vert_values,
    vertical,
    vert_live,
    slash_keys,
    slash_values,
    slash_index,
    slash_live,
):
    tile_count, block_len, head_width = query_tiles.shape
    lane_pos = jnp.arange(block_len, dtype=jnp.int32)
    query_pos = query_index[:, None] * block_len + lane_pos[None, :]
    vert_pos = vertical[:, None] * block_len + lane_pos[None, :]
    slash_pos = slash_index[:, :, None] * block_len + lane_pos[None, None, :]
    score_scale = 1.0 / math.sqrt(head_width)
    vert_scores = (
        jnp.einsum("gid,vjd->givj", query_tiles, vert_keys, preferred_element_type=jnp.float32)
        * score_scale
    )
    slash_scores = (
        jnp.einsum("gid,gsjd->gisj", query_tiles, slash_keys, preferred_element_type=jnp.float32)
        * score_scale
    )
    vert_mask = vert_live[None, None, :, None] & (
        vert_pos[None, None, :, :] <= query_pos[:, :, None, None]
    )
    slash_mask = slash_live[:, None, :, None] & (
        slash_pos[:, None, :, :] <= query_pos[:, :, None, None]
    )
    scores = jnp.concatenate(
        [
            jnp.where(vert_mask, vert_scores, -jnp.inf).reshape(tile_count, block_len, -1),
            jnp.where(slash_mask, slash_scores, -jnp.inf).reshape(tile_count, block_len, -1),
        ],
        axis=2,
    )
    row_max = jnp.max(scores, axis=2, keepdims=True)
    raised = jnp.exp(scores - row_max)
    weights = (raised / jnp.sum(raised, axis=2, keepdims=True)).astype(jnp.bfloat16)
    vert_width = vert_keys.shape[0] * block_len
    result = jnp.einsum(
        "gik,kd->gid",
        weights[:, :, :vert_width],
        vert_values.reshape(vert_width, head_width),
        preferred_element_type=jnp.float32,
    )
    result = result + jnp.einsum(
        "gik,gkd->gid",
        weights[:, :, vert_width:],
        slash_values.reshape(tile_count, -1, head_width),
        preferred_element_type=jnp.float32,
    )
    return result.astype(jnp.bfloat16).reshape(tile_count * block_len, head_width)


def by_head_owner(queries, keys, values, vert_blocks, vert_count, slash_offsets, slash_count):
    owners = lax.axis_size("seq")
    cycle_size = lax.axis_size("blk")
    owner_id = lax.axis_index("seq")
    cycle_id = lax.axis_index("blk")
    shard_rows, head_total, head_width = queries.shape
    kv_total = keys.shape[1]
    group_size = head_total // kv_total
    per_owner = head_total // owners
    kv_owned = max(1, kv_total // owners)
    sharers = max(1, owners // kv_total)
    blocks_per_shard = shard_rows // BLOCK
    query_send = queries.reshape(shard_rows, owners, per_owner, head_width)

    def by_owner(tensor):
        if sharers > 1:
            tensor = jnp.repeat(tensor, sharers, axis=1)
        return tensor.reshape(tensor.shape[0], owners, kv_owned, head_width)

    query_rows, key_part, value_part = (
        lax.all_to_all(query_send, "seq", split_axis=1, concat_axis=0, tiled=True),
        lax.all_to_all(by_owner(keys), "seq", split_axis=1, concat_axis=0, tiled=True),
        lax.all_to_all(by_owner(values), "seq", split_axis=1, concat_axis=0, tiled=True),
    )
    key_rows, value_rows = (
        lax.all_gather(key_part, "blk", axis=0, tiled=True),
        lax.all_gather(value_part, "blk", axis=0, tiled=True),
    )

    def stored(block_id):
        first_row = block_id * BLOCK
        source = first_row // shard_rows
        return (
            source % cycle_size * owners + source // cycle_size
        ) * blocks_per_shard + first_row % shard_rows // BLOCK

    key_heads = jnp.moveaxis(key_rows.reshape(-1, BLOCK, kv_owned, head_width), 2, 0)
    value_heads = jnp.moveaxis(value_rows.reshape(-1, BLOCK, kv_owned, head_width), 2, 0)
    block_total = key_heads.shape[1]
    owned_rows = owners * shard_rows
    group_rows = min(512, owned_rows)
    groups = owned_rows // group_rows
    group_blocks = group_rows // BLOCK
    query_heads = jnp.transpose(query_rows.reshape(owned_rows, per_owner, head_width), (1, 0, 2))

    def attend(step_id):
        slot_id = step_id // groups
        group_id = step_id % groups
        head_id = owner_id * per_owner + slot_id
        kv_local = head_id // group_size - owner_id // sharers * kv_owned
        head_queries = lax.dynamic_index_in_dim(query_heads, slot_id, 0, False)
        query_tiles = lax.dynamic_slice_in_dim(
            head_queries, group_id * group_rows, group_rows, 0
        ).reshape(group_blocks, BLOCK, head_width)
        local_rows = group_id * group_rows + jnp.arange(group_blocks, dtype=jnp.int32) * BLOCK
        query_index = (
            local_rows // shard_rows * cycle_size + cycle_id
        ) * blocks_per_shard + local_rows % shard_rows // BLOCK
        vertical = lax.dynamic_index_in_dim(vert_blocks, head_id, 0, False)
        vert_live = jnp.arange(vertical.shape[0], dtype=jnp.int32) < lax.dynamic_index_in_dim(
            vert_count, head_id, 0, False
        )
        slash = lax.dynamic_index_in_dim(slash_offsets, head_id, 0, False)
        slash_live = jnp.arange(slash.shape[0], dtype=jnp.int32) < lax.dynamic_index_in_dim(
            slash_count, head_id, 0, False
        )
        slash_index, usable = slash_plan(query_index, vertical, vert_live, slash, slash_live)
        clamped = stored(jnp.clip(slash_index, 0, block_total - 1))
        vert_rows = stored(vertical)
        head_keys = lax.dynamic_index_in_dim(key_heads, kv_local, 0, False)
        head_values = lax.dynamic_index_in_dim(value_heads, kv_local, 0, False)
        vert_keys = jnp.take(head_keys, vert_rows, axis=0)
        vert_values = jnp.take(head_values, vert_rows, axis=0)
        slash_keys = jnp.take(head_keys, clamped, axis=0)
        slash_values = jnp.take(head_values, clamped, axis=0)
        return sparse_block(
            query_tiles,
            query_index,
            vert_keys,
            vert_values,
            vertical,
            vert_live,
            slash_keys,
            slash_values,
            slash_index,
            usable,
        )

    attended = lax.map(attend, jnp.arange(per_owner * groups, dtype=jnp.int32))
    attended = attended.reshape(per_owner, owners, shard_rows, head_width)
    returned = lax.all_to_all(attended, "seq", split_axis=1, concat_axis=1, tiled=True)
    return jnp.transpose(returned, (2, 1, 0, 3)).reshape(shard_rows, head_total, head_width)


def listed(entries, live_count, wanted):
    row = lax.broadcasted_iota(jnp.int32, entries.shape, 0)
    hit = (entries == wanted) & (row < live_count)
    return jnp.sum(jnp.where(hit, 1.0, 0.0), axis=0, keepdims=True)

def block_bias(vert, vcount, slash, scount, query_block, key_blocks):
    heads = vert.shape[1]
    rows = []
    for kb in key_blocks:
        n = listed(vert, vcount, kb) + listed(slash, scount, query_block - kb)
        ok = jnp.where((kb >= 0) & (kb <= query_block), 1.0, 0.0)
        rows.append(n * ok)
    taken = jnp.concatenate(rows, axis=0)
    pad = 8 - len(key_blocks)
    if pad:
        taken = jnp.concatenate([taken, jnp.zeros((pad, heads), jnp.float32)], axis=0)
    width = len(key_blocks) * BLOCK
    spread = (
        lax.broadcasted_iota(jnp.int32, (8, width), 0)
        == lax.broadcasted_iota(jnp.int32, (8, width), 1) // BLOCK
    )
    count = lax.dot_general(
        taken, jnp.where(spread, 1.0, 0.0), (((0,), (0,)), ((), ())),
        preferred_element_type=jnp.float32,
    )
    return jnp.where(count > 0.5, 0.0, NEG)

def stage_body(first, last, slots, kv_heads, group, scale, *refs):
    (ids, vert, vcount, slash, scount, q_own, q_sib), refs = refs[:7], refs[7:]
    tiles, refs = refs[:slots], refs[slots:]
    if not first:
        acc_in, top_in, sum_in = refs[:3]
        refs = refs[3:]
    if last:
        out_own, out_sib, bias_ref = refs
    else:
        acc_out, top_out, sum_out, bias_ref = refs
    core = ids[0]
    half = kv_heads * group
    key_blocks = [ids[3 + t] for t in range(slots)]
    for b in range(2):
        bias_ref[b] = block_bias(vert[...], vcount[...], slash[...], scount[...], ids[1 + b], key_blocks)
    lo = pl.multiple_of(core * half, half)
    width = slots * BLOCK
    rows = BLOCK * group
    if first:
        pos = lax.broadcasted_iota(jnp.int32, (BLOCK, 1, 2 * BLOCK), 0)
        key = lax.broadcasted_iota(jnp.int32, (BLOCK, 1, 2 * BLOCK), 2)
    for b in range(2):
        q_ref, o_ref = (q_own, q_sib)[b], ((out_own, out_sib)[b] if last else None)
        for pair in range(kv_heads // 2):
            q16 = q_ref[:, pl.ds(pl.multiple_of(lo + pair * 2 * group, 2 * group), 2 * group), :].astype(jnp.float32)
            outs = []
            for one in range(2):
                g = pair * 2 + one
                q = q16[:, one * group:(one + 1) * group, :].reshape(rows, 128).astype(jnp.bfloat16)
                k = jnp.concatenate([t[0, g] for t in tiles], axis=0)
                v = jnp.concatenate([t[1, g] for t in tiles], axis=0)
                s = lax.dot_general(q, k, (((1,), (1,)), ((), ())), preferred_element_type=jnp.float32)
                s = s.reshape(BLOCK, group, width)
                head = pl.ds(pl.multiple_of(lo + g * group, group), group)
                s = s + bias_ref[b, head, :][None]
                if first:
                    lane_pos = key - b * BLOCK
                    causal = jnp.where((lane_pos > pos) & (lane_pos < BLOCK), NEG, 0.0)
                    s = jnp.concatenate([s[:, :, :128] + causal, s[:, :, 128:]], axis=2)
                s = s.reshape(rows, width)
                top = jnp.broadcast_to(jnp.max(s, axis=1, keepdims=True), (rows, 128))
                if not first:
                    old_top = top_in[b, g]
                    top = jnp.maximum(top, old_top)
                    shrink = jnp.exp2((old_top - top) * scale)
                p = jnp.exp2((s - jnp.concatenate([top] * (width // 128), axis=1)) * scale)
                total = jnp.broadcast_to(jnp.sum(p, axis=1, keepdims=True), (rows, 128))
                acc = jnp.dot(p.astype(jnp.bfloat16), v, preferred_element_type=jnp.float32)
                if not first:
                    total = total + sum_in[b, g] * shrink
                    acc = acc + acc_in[b, g] * shrink
                if last:
                    outs.append((acc / total).reshape(BLOCK, group, 128))
                else:
                    acc_out[b, g] = acc
                    top_out[b, g] = top
                    sum_out[b, g] = total
            if last:
                o_ref[:, pair * 2 * group:(pair + 1) * 2 * group, :] = jnp.concatenate(outs, axis=1).astype(jnp.bfloat16)

def attend_stage(ids, patterns, q_own, q_sib, tiles, state, last):
    _, kv_heads, _, width = tiles[0].shape
    heads = q_own.shape[1]
    half = heads // 2
    group = half // kv_heads
    rows = BLOCK * group
    first = state is None
    scale = 1.0 / math.sqrt(width) * math.log2(math.e)
    vm = pl.BlockSpec(memory_space=pltpu.VMEM)
    args = [ids, *patterns, q_own, q_sib, *tiles] + ([] if first else list(state))
    specs = [pl.BlockSpec(memory_space=pltpu.SMEM)] + [vm] * (len(args) - 1)
    if last:
        out = [jax.ShapeDtypeStruct((BLOCK, half, width), jnp.bfloat16)] * 2
    else:
        out = [jax.ShapeDtypeStruct((2, kv_heads, rows, width), jnp.float32)] * 3

    flops = 4 * 2 * half * BLOCK * BLOCK * len(tiles) * width
    return pl.pallas_call(
        functools.partial(stage_body, first, last, len(tiles), kv_heads, group, scale),
        out_shape=out,
        in_specs=specs,
        out_specs=[vm] * len(out),
        scratch_shapes=[pltpu.VMEM((2, heads, BLOCK * len(tiles)), jnp.float32)],
        compiler_params=pltpu.CompilerParams(vmem_limit_bytes=32 * 1024 * 1024),
        cost_estimate=pl.CostEstimate(flops=flops, bytes_accessed=4 << 20, transcendentals=flops // (4 * width)),
        name="attend",
    )(*args)


def split_body(core_ref, k_ref, v_ref, keep_ref, give_ref, turned):
    half = k_ref.shape[1] // 2
    for which, ref in enumerate((k_ref, v_ref)):
        turned[which] = jnp.swapaxes(ref[...].astype(jnp.float32), 0, 1).astype(jnp.bfloat16)
    core = core_ref[0]
    keep_ref[...] = turned[:, pl.ds(core * half, half)]
    give_ref[...] = turned[:, pl.ds((1 - core) * half, half)]


def split_heads(core, keys, values):
    rows, kv_total, width = keys.shape
    vm = pl.BlockSpec(memory_space=pltpu.VMEM)
    half = jax.ShapeDtypeStruct((2, kv_total // 2, rows, width), jnp.bfloat16)
    return pl.pallas_call(
        split_body,
        out_shape=[half, half],
        in_specs=[pl.BlockSpec(memory_space=pltpu.SMEM), vm, vm],
        out_specs=[vm, vm],
        scratch_shapes=[pltpu.VMEM((2, kv_total, rows, width), jnp.bfloat16)],
        compiler_params=pltpu.CompilerParams(vmem_limit_bytes=8 * 1024 * 1024),
        cost_estimate=pl.CostEstimate(flops=0, bytes_accessed=512 * 1024, transcendentals=0),
        name="split",
    )(core, keys, values)


def join_body(core_ref, mine_ref, other_ref, out_ref):
    half = mine_ref.shape[1]
    core = core_ref[0]
    out_ref[:, pl.ds(pl.multiple_of(core * half, half), half), :] = mine_ref[...]
    out_ref[:, pl.ds(pl.multiple_of((1 - core) * half, half), half), :] = other_ref[...]


def join_heads(core, mine, other):
    rows, half, width = mine.shape
    vm = pl.BlockSpec(memory_space=pltpu.VMEM)
    return pl.pallas_call(
        join_body,
        out_shape=jax.ShapeDtypeStruct((rows, 2 * half, width), jnp.bfloat16),
        in_specs=[pl.BlockSpec(memory_space=pltpu.SMEM), vm, vm],
        out_specs=vm,
        compiler_params=pltpu.CompilerParams(vmem_limit_bytes=8 * 1024 * 1024),
        cost_estimate=pl.CostEstimate(flops=0, bytes_accessed=2 << 20, transcendentals=0),
        name="join",
    )(core, mine, other)


def by_key_block(queries, keys, values, vert_blocks, vert_count, slash_offsets, slash_count):
    planes = lax.axis_size("seq")
    plane = lax.axis_index("seq")
    place = lax.axis_index("blk")
    core, column = place % 2, place // 2
    up = [(i, i + 1) for i in range(planes - 1)]

    def climb(tile):
        return lax.ppermute(tile, "seq", up)

    def across(tile):
        return lax.ppermute(tile, "blk", [(0, 2), (2, 0), (1, 3), (3, 1)])

    def sibling(tile):
        return lax.ppermute(tile, "blk", [(0, 1), (1, 0), (2, 3), (3, 2)])

    core_id = core[None]
    keep, give = split_heads(core_id, keys, values)
    patterns = (vert_blocks.T, vert_count[None], slash_offsets.T, slash_count[None])
    mine, theirs = keep, sibling(give)
    sibling_queries = sibling(queries)
    state = None
    slots = jnp.stack([2 * column + core, 2 * column + 1 - core, 2 * (1 - column) + core, 2 * (1 - column) + 1 - core])
    own_ids = jnp.stack([core, plane * 4 + slots[0], plane * 4 + slots[1]])
    for stage in range(planes):
        tiles = [mine, theirs, across(mine), across(theirs)]
        ids = jnp.concatenate([own_ids, (plane - stage) * 4 + slots])
        last = stage == planes - 1
        state = attend_stage(ids, patterns, queries, sibling_queries, tiles, state, last)
        if not last:
            mine, theirs = climb(mine), climb(theirs)
    own_rows, sibling_rows = state
    return join_heads(core_id, own_rows, sibling(sibling_rows))


def on_device(queries, keys, values, vert_blocks, vert_count, slash_offsets, slash_count):
    gathered = 2 * keys.size * keys.dtype.itemsize * lax.axis_size("seq") * lax.axis_size("blk")
    fits = gathered <= GATHER_BYTES and keys.shape[0] == BLOCK and lax.axis_size("blk") == 4
    plan = by_key_block if fits else by_head_owner
    return plan(queries, keys, values, vert_blocks, vert_count, slash_offsets, slash_count)


def solution(mesh):
    return jax.shard_map(
        on_device,
        mesh=mesh,
        in_specs=(
            P(("grp", "seq", "blk"), None, None),
            P(("grp", "seq", "blk"), None, None),
            P(("grp", "seq", "blk"), None, None),
            P(),
            P(),
            P(),
            P(),
        ),
        out_specs=P(("grp", "seq", "blk"), None, None),
        check_vma=False,
    )
```

```python
import functools
import math

import jax
import jax.numpy as jnp
from jax import lax
from jax.experimental import pallas as pl
from jax.experimental.pallas import tpu as pltpu
from jax.sharding import PartitionSpec as P

BLOCK = 64
NEG = -1e30
GATHER_BYTES = 8 << 20


def slash_plan(query_index, vertical, vert_live, slash, slash_live):
    slash_index = query_index[:, None] - slash[None, :]
    duplicate = jnp.any(
        (slash_index[:, :, None] == vertical[None, None, :]) & vert_live[None, None, :], axis=2
    )
    usable = slash_live[None, :] & (slash_index >= 0) & jnp.logical_not(duplicate)
    return (slash_index, usable)


def sparse_block(
    query_tiles,
    query_index,
    vert_keys,
    vert_values,
    vertical,
    vert_live,
    slash_keys,
    slash_values,
    slash_index,
    slash_live,
):
    tile_count, block_len, head_width = query_tiles.shape
    lane_pos = jnp.arange(block_len, dtype=jnp.int32)
    query_pos = query_index[:, None] * block_len + lane_pos[None, :]
    vert_pos = vertical[:, None] * block_len + lane_pos[None, :]
    slash_pos = slash_index[:, :, None] * block_len + lane_pos[None, None, :]
    score_scale = 1.0 / math.sqrt(head_width)
    vert_scores = (
        jnp.einsum("gid,vjd->givj", query_tiles, vert_keys, preferred_element_type=jnp.float32)
        * score_scale
    )
    slash_scores = (
        jnp.einsum("gid,gsjd->gisj", query_tiles, slash_keys, preferred_element_type=jnp.float32)
        * score_scale
    )
    vert_mask = vert_live[None, None, :, None] & (
        vert_pos[None, None, :, :] <= query_pos[:, :, None, None]
    )
    slash_mask = slash_live[:, None, :, None] & (
        slash_pos[:, None, :, :] <= query_pos[:, :, None, None]
    )
    scores = jnp.concatenate(
        [
            jnp.where(vert_mask, vert_scores, -jnp.inf).reshape(tile_count, block_len, -1),
            jnp.where(slash_mask, slash_scores, -jnp.inf).reshape(tile_count, block_len, -1),
        ],
        axis=2,
    )
    row_max = jnp.max(scores, axis=2, keepdims=True)
    raised = jnp.exp(scores - row_max)
    weights = (raised / jnp.sum(raised, axis=2, keepdims=True)).astype(jnp.bfloat16)
    vert_width = vert_keys.shape[0] * block_len
    result = jnp.einsum(
        "gik,kd->gid",
        weights[:, :, :vert_width],
        vert_values.reshape(vert_width, head_width),
        preferred_element_type=jnp.float32,
    )
    result = result + jnp.einsum(
        "gik,gkd->gid",
        weights[:, :, vert_width:],
        slash_values.reshape(tile_count, -1, head_width),
        preferred_element_type=jnp.float32,
    )
    return result.astype(jnp.bfloat16).reshape(tile_count * block_len, head_width)


def by_head_owner(queries, keys, values, vert_blocks, vert_count, slash_offsets, slash_count):
    owners = lax.axis_size("seq")
    cycle_size = lax.axis_size("blk")
    owner_id = lax.axis_index("seq")
    cycle_id = lax.axis_index("blk")
    shard_rows, head_total, head_width = queries.shape
    kv_total = keys.shape[1]
    group_size = head_total // kv_total
    per_owner = head_total // owners
    kv_owned = max(1, kv_total // owners)
    sharers = max(1, owners // kv_total)
    blocks_per_shard = shard_rows // BLOCK
    query_send = queries.reshape(shard_rows, owners, per_owner, head_width)

    def by_owner(tensor):
        if sharers > 1:
            tensor = jnp.repeat(tensor, sharers, axis=1)
        return tensor.reshape(tensor.shape[0], owners, kv_owned, head_width)

    query_rows, key_part, value_part = (
        lax.all_to_all(query_send, "seq", split_axis=1, concat_axis=0, tiled=True),
        lax.all_to_all(by_owner(keys), "seq", split_axis=1, concat_axis=0, tiled=True),
        lax.all_to_all(by_owner(values), "seq", split_axis=1, concat_axis=0, tiled=True),
    )
    key_rows, value_rows = (
        lax.all_gather(key_part, "blk", axis=0, tiled=True),
        lax.all_gather(value_part, "blk", axis=0, tiled=True),
    )

    def stored(block_id):
        first_row = block_id * BLOCK
        source = first_row // shard_rows
        return (
            source % cycle_size * owners + source // cycle_size
        ) * blocks_per_shard + first_row % shard_rows // BLOCK

    key_heads = jnp.moveaxis(key_rows.reshape(-1, BLOCK, kv_owned, head_width), 2, 0)
    value_heads = jnp.moveaxis(value_rows.reshape(-1, BLOCK, kv_owned, head_width), 2, 0)
    block_total = key_heads.shape[1]
    owned_rows = owners * shard_rows
    group_rows = min(512, owned_rows)
    groups = owned_rows // group_rows
    group_blocks = group_rows // BLOCK
    query_heads = jnp.transpose(query_rows.reshape(owned_rows, per_owner, head_width), (1, 0, 2))

    def attend(step_id):
        slot_id = step_id // groups
        group_id = step_id % groups
        head_id = owner_id * per_owner + slot_id
        kv_local = head_id // group_size - owner_id // sharers * kv_owned
        head_queries = lax.dynamic_index_in_dim(query_heads, slot_id, 0, False)
        query_tiles = lax.dynamic_slice_in_dim(
            head_queries, group_id * group_rows, group_rows, 0
        ).reshape(group_blocks, BLOCK, head_width)
        local_rows = group_id * group_rows + jnp.arange(group_blocks, dtype=jnp.int32) * BLOCK
        query_index = (
            local_rows // shard_rows * cycle_size + cycle_id
        ) * blocks_per_shard + local_rows % shard_rows // BLOCK
        vertical = lax.dynamic_index_in_dim(vert_blocks, head_id, 0, False)
        vert_live = jnp.arange(vertical.shape[0], dtype=jnp.int32) < lax.dynamic_index_in_dim(
            vert_count, head_id, 0, False
        )
        slash = lax.dynamic_index_in_dim(slash_offsets, head_id, 0, False)
        slash_live = jnp.arange(slash.shape[0], dtype=jnp.int32) < lax.dynamic_index_in_dim(
            slash_count, head_id, 0, False
        )
        slash_index, usable = slash_plan(query_index, vertical, vert_live, slash, slash_live)
        clamped = stored(jnp.clip(slash_index, 0, block_total - 1))
        vert_rows = stored(vertical)
        head_keys = lax.dynamic_index_in_dim(key_heads, kv_local, 0, False)
        head_values = lax.dynamic_index_in_dim(value_heads, kv_local, 0, False)
        vert_keys = jnp.take(head_keys, vert_rows, axis=0)
        vert_values = jnp.take(head_values, vert_rows, axis=0)
        slash_keys = jnp.take(head_keys, clamped, axis=0)
        slash_values = jnp.take(head_values, clamped, axis=0)
        return sparse_block(
            query_tiles,
            query_index,
            vert_keys,
            vert_values,
            vertical,
            vert_live,
            slash_keys,
            slash_values,
            slash_index,
            usable,
        )

    attended = lax.map(attend, jnp.arange(per_owner * groups, dtype=jnp.int32))
    attended = attended.reshape(per_owner, owners, shard_rows, head_width)
    returned = lax.all_to_all(attended, "seq", split_axis=1, concat_axis=1, tiled=True)
    return jnp.transpose(returned, (2, 1, 0, 3)).reshape(shard_rows, head_total, head_width)


def listed(entries, live_count, wanted):
    row = lax.broadcasted_iota(jnp.int32, entries.shape, 0)
    hit = (entries == wanted) & (row < live_count)
    return jnp.sum(jnp.where(hit, 1.0, 0.0), axis=0, keepdims=True)

def pattern_body(stages, vert_rows, slash_rows, ids, lists, out_ref, taken_ref):
    vert, vcount = lists[:vert_rows], lists[vert_rows:vert_rows + 1]
    slash, scount = lists[vert_rows + 1:vert_rows + 1 + slash_rows], lists[vert_rows + 1 + slash_rows:]
    half = out_ref.shape[2]
    slots = out_ref.shape[3] // BLOCK
    lo = pl.multiple_of(ids[0] * half, half)
    spread = (
        lax.broadcasted_iota(jnp.int32, (8, slots * BLOCK), 0)
        == lax.broadcasted_iota(jnp.int32, (8, slots * BLOCK), 1) // BLOCK
    )
    spread = jnp.where(spread, 1.0, 0.0)
    pad = jnp.zeros((8 - slots, lists.shape[1]), jnp.float32)
    for stage in range(stages):
        for b in range(2):
            rows = []
            for slot in range(slots):
                key_block, query_block = ids[3 + stage * slots + slot], ids[1 + b]
                n = listed(vert, vcount, key_block) + listed(slash, scount, query_block - key_block)
                rows.append(n * jnp.where((key_block >= 0) & (key_block <= query_block), 1.0, 0.0))
            taken = lax.dot_general(
                jnp.concatenate(rows + [pad], axis=0),
                spread,
                (((0,), (0,)), ((), ())),
                preferred_element_type=jnp.float32,
            )
            taken_ref[...] = jnp.where(taken > 0.5, 0.0, NEG)
            out_ref[stage, b] = taken_ref[pl.ds(lo, half), :]


def pattern_bias(ids, stages, slots, vert_rows, slash_rows, lists):
    heads = lists.shape[1]
    vm = pl.BlockSpec(memory_space=pltpu.VMEM)
    return pl.pallas_call(
        functools.partial(pattern_body, stages, vert_rows, slash_rows),
        out_shape=jax.ShapeDtypeStruct((stages, 2, heads // 2, slots * BLOCK), jnp.float32),
        in_specs=[pl.BlockSpec(memory_space=pltpu.SMEM), vm],
        out_specs=vm,
        scratch_shapes=[pltpu.VMEM((heads, slots * BLOCK), jnp.float32)],
        compiler_params=pltpu.CompilerParams(vmem_limit_bytes=8 * 1024 * 1024),
        cost_estimate=pl.CostEstimate(flops=1000, bytes_accessed=1000, transcendentals=0),
        name="pattern",
    )(ids, lists)


def stage_body(stage, rows_of, slots, group, scale, *refs):
    last = rows_of is not None
    (bias, q_own, q_sib), refs = refs[:3], refs[3:]
    tiles, refs = refs[:slots], refs[slots:]
    first = stage == 0
    if not first:
        acc_in, top_in, sum_in = refs[:3]
        refs = refs[3:]
    if last:
        core, out, *refs = refs
        done_ref, *sems = refs if rows_of == "own" else (out,)
    else:
        acc_out, top_out, sum_out = refs
    kv_heads, rows, head_width = q_own.shape
    width = slots * BLOCK
    if first:
        pos = lax.broadcasted_iota(jnp.int32, (BLOCK, 1, 2 * BLOCK), 0)
        key = lax.broadcasted_iota(jnp.int32, (BLOCK, 1, 2 * BLOCK), 2)
    for b in {None: (0, 1), "own": (0,), "sibling": (1,)}[rows_of]:
        q_ref = (q_own, q_sib)[b]
        outs = []
        for g in range(kv_heads):
            k = jnp.concatenate([t[0, g] for t in tiles], axis=0)
            v = jnp.concatenate([t[1, g] for t in tiles], axis=0)
            s = lax.dot_general(q_ref[g], k, (((1,), (1,)), ((), ())), preferred_element_type=jnp.float32)
            s = s.reshape(BLOCK, group, width) + bias[stage, b, g * group:(g + 1) * group, :][None]
            if first:
                offset = key - b * BLOCK
                causal = jnp.where((offset > pos) & (offset < BLOCK), NEG, 0.0)
                s = jnp.concatenate([s[:, :, :2 * BLOCK] + causal, s[:, :, 2 * BLOCK:]], axis=2)
            s = s.reshape(rows, width)
            top = jnp.broadcast_to(jnp.max(s, axis=1, keepdims=True), (rows, head_width))
            if not first:
                old_top = top_in[b, g]
                top = jnp.maximum(top, old_top)
                shrink = jnp.exp2((old_top - top) * scale)
            p = jnp.exp2((s - jnp.concatenate([top] * (width // head_width), axis=1)) * scale)
            total = jnp.broadcast_to(jnp.sum(p, axis=1, keepdims=True), (rows, head_width))
            acc = jnp.dot(p.astype(jnp.bfloat16), v, preferred_element_type=jnp.float32)
            if not first:
                total = total + sum_in[b, g] * shrink
                acc = acc + acc_in[b, g] * shrink
            if not last:
                acc_out[b, g] = acc
                top_out[b, g] = top
                sum_out[b, g] = total
                continue
            outs.append((acc / total).reshape(BLOCK, group, head_width))
            if g % 2:
                pair = jnp.concatenate(outs, axis=1).astype(jnp.bfloat16)
                done_ref[:, (g - 1) * group:(g + 1) * group, :] = pair
                outs = []
    if last and rows_of == "own":
        half = kv_heads * group
        place = pl.ds(pl.multiple_of(core[0] * half, half), half)
        send = pltpu.make_async_copy(done_ref, out.at[:, place, :], sems[0])
        send.start()
        send.wait()


def attend_stage(stage, bias, q_own, q_sib, tiles, state, rows_of=None, core=None):
    kv_heads, rows, head_width = q_own.shape
    group = rows // BLOCK
    scale = 1.0 / math.sqrt(head_width) * math.log2(math.e)
    vm = pl.BlockSpec(memory_space=pltpu.VMEM)
    args = [bias, q_own, q_sib, *tiles, *state]
    specs, scratch = [vm] * len(args), []
    half = (BLOCK, kv_heads * group, head_width)
    if rows_of is None:
        out = [jax.ShapeDtypeStruct((2, kv_heads, rows, head_width), jnp.float32)] * 3
        out_specs = [vm] * 3
    else:
        args, specs = args + [core], specs + [pl.BlockSpec(memory_space=pltpu.SMEM)]
        out, out_specs = jax.ShapeDtypeStruct(half, jnp.bfloat16), vm
        if rows_of == "own":
            out = jax.ShapeDtypeStruct((BLOCK, 2 * half[1], head_width), jnp.bfloat16)
            out_specs = pl.BlockSpec(memory_space=pl.ANY)
            scratch = [pltpu.VMEM(half, jnp.bfloat16), pltpu.SemaphoreType.DMA]
    return pl.pallas_call(
        functools.partial(stage_body, stage, rows_of, len(tiles), group, scale),
        out_shape=out,
        in_specs=specs,
        out_specs=out_specs,
        scratch_shapes=scratch,
        compiler_params=pltpu.CompilerParams(vmem_limit_bytes=16 * 1024 * 1024),
        cost_estimate=pl.CostEstimate(flops=1000, bytes_accessed=1000, transcendentals=0),
        name="attend",
    )(*args)


def turn_body(core_ref, q_own, q_sib, own_ref, sib_ref):
    kv_half, rows, width = own_ref.shape
    group = rows // BLOCK
    for q_ref, out in ((q_own, own_ref), (q_sib, sib_ref)):
        for pair in range(kv_half // 2):
            lo = pl.multiple_of((core_ref[0] * kv_half + pair * 2) * group, 2 * group)
            both = q_ref[:, pl.ds(lo, 2 * group), :].astype(jnp.float32)
            for one in range(2):
                mine = both[:, one * group:(one + 1) * group, :].reshape(rows, width)
                out[pair * 2 + one] = mine.astype(jnp.bfloat16)


def turn_queries(core, own, sib, kv_total):
    positions, heads, width = own.shape
    vm = pl.BlockSpec(memory_space=pltpu.VMEM)
    half = jax.ShapeDtypeStruct((kv_total // 2, positions * heads // kv_total, width), jnp.bfloat16)
    return pl.pallas_call(
        turn_body,
        out_shape=[half, half],
        in_specs=[pl.BlockSpec(memory_space=pltpu.SMEM), vm, vm],
        out_specs=[vm, vm],
        compiler_params=pltpu.CompilerParams(vmem_limit_bytes=8 * 1024 * 1024),
        cost_estimate=pl.CostEstimate(flops=1000, bytes_accessed=1000, transcendentals=0),
        name="turn",
    )(core, own, sib)


def split_body(core_ref, k_hbm, v_hbm, keep_ref, give_ref, raw, turned, sems):
    half = turned.shape[1] // 2
    fetches = [pltpu.make_async_copy(hbm, raw.at[n], sems.at[n]) for n, hbm in enumerate((k_hbm, v_hbm))]
    for fetch in fetches:
        fetch.start()
    core = core_ref[0]
    for n, fetch in enumerate(fetches):
        fetch.wait()
        turned[n] = jnp.swapaxes(raw[n].astype(jnp.float32), 0, 1).astype(jnp.bfloat16)
    keep_ref[...] = turned[:, pl.ds(core * half, half)]
    give_ref[...] = turned[:, pl.ds((1 - core) * half, half)]


def split_heads(core, keys, values):
    rows, kv_total, width = keys.shape
    vm, hbm = pl.BlockSpec(memory_space=pltpu.VMEM), pl.BlockSpec(memory_space=pltpu.HBM)
    half = jax.ShapeDtypeStruct((2, kv_total // 2, rows, width), jnp.bfloat16)
    return pl.pallas_call(
        split_body,
        out_shape=[half, half],
        in_specs=[pl.BlockSpec(memory_space=pltpu.SMEM), hbm, hbm],
        out_specs=[vm, vm],
        scratch_shapes=[
            pltpu.VMEM((2, rows, kv_total, width), jnp.bfloat16),
            pltpu.VMEM((2, kv_total, rows, width), jnp.bfloat16),
            pltpu.SemaphoreType.DMA((2,)),
        ],
        compiler_params=pltpu.CompilerParams(vmem_limit_bytes=60 * 1024 * 1024),
        cost_estimate=pl.CostEstimate(flops=1000, bytes_accessed=1000, transcendentals=0),
        name="split",
    )(core, keys, values)


def join_body(core_ref, other_ref, begun_ref, out_ref, sem):
    half = other_ref.shape[1]
    place = pl.ds(pl.multiple_of((1 - core_ref[0]) * half, half), half)
    send = pltpu.make_async_copy(other_ref, out_ref.at[:, place, :], sem)
    send.start()
    send.wait()


def join_heads(core, other, begun):
    somewhere = pl.BlockSpec(memory_space=pl.ANY)
    return pl.pallas_call(
        join_body,
        out_shape=jax.ShapeDtypeStruct(begun.shape, begun.dtype),
        in_specs=[pl.BlockSpec(memory_space=pltpu.SMEM), pl.BlockSpec(memory_space=pltpu.VMEM), somewhere],
        out_specs=somewhere,
        scratch_shapes=[pltpu.SemaphoreType.DMA],
        input_output_aliases={2: 0},
        compiler_params=pltpu.CompilerParams(vmem_limit_bytes=8 * 1024 * 1024),
        cost_estimate=pl.CostEstimate(flops=1000, bytes_accessed=1000, transcendentals=0),
        name="join",
    )(core, other, begun)


def by_key_block(queries, keys, values, vert_blocks, vert_count, slash_offsets, slash_count):
    planes = lax.axis_size("seq")
    plane = lax.axis_index("seq")
    place = lax.axis_index("blk")
    core, column = place % 2, place // 2

    def trade(tile, step):
        return lax.ppermute(tile, "seq", [(i, i ^ step) for i in range(planes)])

    def across(tile):
        return lax.ppermute(tile, "blk", [(0, 2), (2, 0), (1, 3), (3, 1)])

    def sibling(tile):
        return lax.ppermute(tile, "blk", [(0, 1), (1, 0), (2, 3), (3, 2)])

    core_id = core[None]
    sibling_queries = sibling(queries)
    keep, give = split_heads(core_id, keys, values)
    slots = jnp.stack([2 * column + core, 2 * column + 1 - core, 2 * (1 - column) + core, 2 * (1 - column) + 1 - core])
    ids = jnp.concatenate(
        [jnp.stack([core, plane * 4 + slots[0], plane * 4 + slots[1]])]
        + [(plane ^ step) * 4 + slots for step in (0, 1, 3, 2)]
    )
    a, b = keep, sibling(give)
    far_a, x_a, near_a = trade(a, 3), across(a), trade(a, 1)
    b, queries_b = lax.optimization_barrier((b, sibling_queries))
    far_b = trade(b, 3)
    q_keep, q_sib = turn_queries(core_id, queries, queries_b, 2 * give.shape[1])
    lists = jnp.concatenate([vert_blocks.T, vert_count[None], slash_offsets.T, slash_count[None]])
    bias = pattern_bias(ids, planes, 4, vert_blocks.shape[1], slash_offsets.shape[1], lists)
    x_b = across(b)
    late_b, near_a, bias, q_keep, q_sib = lax.optimization_barrier((b, near_a, bias, q_keep, q_sib))
    near_b = trade(late_b, 1)
    x_near_a = across(near_a)
    far_a, q_sib, bias, x_b = lax.optimization_barrier((far_a, q_sib, bias, x_b))
    last_a = trade(far_a, 1)
    x_far_a = across(far_a)
    x_near_b = across(near_b)
    state = attend_stage(0, bias, q_keep, q_sib, [a, b, x_a, x_b], ())
    far_b, state = lax.optimization_barrier((far_b, state))
    last_b = trade(far_b, 1)
    x_far_b = across(far_b)
    state = attend_stage(1, bias, q_keep, q_sib, [near_a, near_b, x_near_a, x_near_b], state)
    go_b, state = lax.optimization_barrier((last_b, state))
    x_last_a, x_last_b = trade(x_far_a, 1), across(go_b)
    state = attend_stage(2, bias, q_keep, q_sib, [far_a, far_b, x_far_a, x_far_b], state)
    tiles = [last_a, last_b, x_last_a, x_last_b]
    sibling_rows = attend_stage(3, bias, q_keep, q_sib, tiles, state, "sibling", core_id)
    state, sibling_rows = lax.optimization_barrier((state, sibling_rows))
    own_rows = attend_stage(3, bias, q_keep, q_sib, tiles, state, "own", core_id)
    return join_heads(core_id, sibling(sibling_rows), own_rows)


def on_device(queries, keys, values, vert_blocks, vert_count, slash_offsets, slash_count):
    gathered = 2 * keys.size * keys.dtype.itemsize * lax.axis_size("seq") * lax.axis_size("blk")
    fits = gathered <= GATHER_BYTES and keys.shape[0] == BLOCK and lax.axis_size("blk") == 4
    plan = by_key_block if fits else by_head_owner
    return plan(queries, keys, values, vert_blocks, vert_count, slash_offsets, slash_count)


def solution(mesh):
    return jax.shard_map(
        on_device,
        mesh=mesh,
        in_specs=(
            P(("grp", "seq", "blk"), None, None),
            P(("grp", "seq", "blk"), None, None),
            P(("grp", "seq", "blk"), None, None),
            P(),
            P(),
            P(),
            P(),
        ),
        out_specs=P(("grp", "seq", "blk"), None, None),
        check_vma=False,
    )
```

```python
import functools
import math

import jax
import jax.numpy as jnp
from jax import lax
from jax.experimental import pallas as pl
from jax.experimental.pallas import tpu as pltpu
from jax.sharding import PartitionSpec as P

BLOCK = 64
NEG = -1e30
GATHER_BYTES = 8 << 20


def slash_plan(query_index, vertical, vert_live, slash, slash_live):
    slash_index = query_index[:, None] - slash[None, :]
    duplicate = jnp.any(
        (slash_index[:, :, None] == vertical[None, None, :]) & vert_live[None, None, :], axis=2
    )
    usable = slash_live[None, :] & (slash_index >= 0) & jnp.logical_not(duplicate)
    return (slash_index, usable)


def sparse_block(
    query_tiles,
    query_index,
    vert_keys,
    vert_values,
    vertical,
    vert_live,
    slash_keys,
    slash_values,
    slash_index,
    slash_live,
):
    tile_count, block_len, head_width = query_tiles.shape
    lane_pos = jnp.arange(block_len, dtype=jnp.int32)
    query_pos = query_index[:, None] * block_len + lane_pos[None, :]
    vert_pos = vertical[:, None] * block_len + lane_pos[None, :]
    slash_pos = slash_index[:, :, None] * block_len + lane_pos[None, None, :]
    score_scale = 1.0 / math.sqrt(head_width)
    vert_scores = (
        jnp.einsum("gid,vjd->givj", query_tiles, vert_keys, preferred_element_type=jnp.float32)
        * score_scale
    )
    slash_scores = (
        jnp.einsum("gid,gsjd->gisj", query_tiles, slash_keys, preferred_element_type=jnp.float32)
        * score_scale
    )
    vert_mask = vert_live[None, None, :, None] & (
        vert_pos[None, None, :, :] <= query_pos[:, :, None, None]
    )
    slash_mask = slash_live[:, None, :, None] & (
        slash_pos[:, None, :, :] <= query_pos[:, :, None, None]
    )
    scores = jnp.concatenate(
        [
            jnp.where(vert_mask, vert_scores, -jnp.inf).reshape(tile_count, block_len, -1),
            jnp.where(slash_mask, slash_scores, -jnp.inf).reshape(tile_count, block_len, -1),
        ],
        axis=2,
    )
    row_max = jnp.max(scores, axis=2, keepdims=True)
    raised = jnp.exp(scores - row_max)
    weights = (raised / jnp.sum(raised, axis=2, keepdims=True)).astype(jnp.bfloat16)
    vert_width = vert_keys.shape[0] * block_len
    result = jnp.einsum(
        "gik,kd->gid",
        weights[:, :, :vert_width],
        vert_values.reshape(vert_width, head_width),
        preferred_element_type=jnp.float32,
    )
    result = result + jnp.einsum(
        "gik,gkd->gid",
        weights[:, :, vert_width:],
        slash_values.reshape(tile_count, -1, head_width),
        preferred_element_type=jnp.float32,
    )
    return result.astype(jnp.bfloat16).reshape(tile_count * block_len, head_width)


def by_head_owner(queries, keys, values, vert_blocks, vert_count, slash_offsets, slash_count):
    owners = lax.axis_size("seq")
    cycle_size = lax.axis_size("blk")
    owner_id = lax.axis_index("seq")
    cycle_id = lax.axis_index("blk")
    shard_rows, head_total, head_width = queries.shape
    kv_total = keys.shape[1]
    group_size = head_total // kv_total
    per_owner = head_total // owners
    kv_owned = max(1, kv_total // owners)
    sharers = max(1, owners // kv_total)
    blocks_per_shard = shard_rows // BLOCK
    query_send = queries.reshape(shard_rows, owners, per_owner, head_width)

    def by_owner(tensor):
        if sharers > 1:
            tensor = jnp.repeat(tensor, sharers, axis=1)
        return tensor.reshape(tensor.shape[0], owners, kv_owned, head_width)

    query_rows, key_part, value_part = (
        lax.all_to_all(query_send, "seq", split_axis=1, concat_axis=0, tiled=True),
        lax.all_to_all(by_owner(keys), "seq", split_axis=1, concat_axis=0, tiled=True),
        lax.all_to_all(by_owner(values), "seq", split_axis=1, concat_axis=0, tiled=True),
    )
    key_rows, value_rows = (
        lax.all_gather(key_part, "blk", axis=0, tiled=True),
        lax.all_gather(value_part, "blk", axis=0, tiled=True),
    )

    def stored(block_id):
        first_row = block_id * BLOCK
        source = first_row // shard_rows
        return (
            source % cycle_size * owners + source // cycle_size
        ) * blocks_per_shard + first_row % shard_rows // BLOCK

    key_heads = jnp.moveaxis(key_rows.reshape(-1, BLOCK, kv_owned, head_width), 2, 0)
    value_heads = jnp.moveaxis(value_rows.reshape(-1, BLOCK, kv_owned, head_width), 2, 0)
    block_total = key_heads.shape[1]
    owned_rows = owners * shard_rows
    group_rows = min(512, owned_rows)
    groups = owned_rows // group_rows
    group_blocks = group_rows // BLOCK
    query_heads = jnp.transpose(query_rows.reshape(owned_rows, per_owner, head_width), (1, 0, 2))

    def attend(step_id):
        slot_id = step_id // groups
        group_id = step_id % groups
        head_id = owner_id * per_owner + slot_id
        kv_local = head_id // group_size - owner_id // sharers * kv_owned
        head_queries = lax.dynamic_index_in_dim(query_heads, slot_id, 0, False)
        query_tiles = lax.dynamic_slice_in_dim(
            head_queries, group_id * group_rows, group_rows, 0
        ).reshape(group_blocks, BLOCK, head_width)
        local_rows = group_id * group_rows + jnp.arange(group_blocks, dtype=jnp.int32) * BLOCK
        query_index = (
            local_rows // shard_rows * cycle_size + cycle_id
        ) * blocks_per_shard + local_rows % shard_rows // BLOCK
        vertical = lax.dynamic_index_in_dim(vert_blocks, head_id, 0, False)
        vert_live = jnp.arange(vertical.shape[0], dtype=jnp.int32) < lax.dynamic_index_in_dim(
            vert_count, head_id, 0, False
        )
        slash = lax.dynamic_index_in_dim(slash_offsets, head_id, 0, False)
        slash_live = jnp.arange(slash.shape[0], dtype=jnp.int32) < lax.dynamic_index_in_dim(
            slash_count, head_id, 0, False
        )
        slash_index, usable = slash_plan(query_index, vertical, vert_live, slash, slash_live)
        clamped = stored(jnp.clip(slash_index, 0, block_total - 1))
        vert_rows = stored(vertical)
        head_keys = lax.dynamic_index_in_dim(key_heads, kv_local, 0, False)
        head_values = lax.dynamic_index_in_dim(value_heads, kv_local, 0, False)
        vert_keys = jnp.take(head_keys, vert_rows, axis=0)
        vert_values = jnp.take(head_values, vert_rows, axis=0)
        slash_keys = jnp.take(head_keys, clamped, axis=0)
        slash_values = jnp.take(head_values, clamped, axis=0)
        return sparse_block(
            query_tiles,
            query_index,
            vert_keys,
            vert_values,
            vertical,
            vert_live,
            slash_keys,
            slash_values,
            slash_index,
            usable,
        )

    attended = lax.map(attend, jnp.arange(per_owner * groups, dtype=jnp.int32))
    attended = attended.reshape(per_owner, owners, shard_rows, head_width)
    returned = lax.all_to_all(attended, "seq", split_axis=1, concat_axis=1, tiled=True)
    return jnp.transpose(returned, (2, 1, 0, 3)).reshape(shard_rows, head_total, head_width)


def listed(entries, live_count, wanted):
    row = lax.broadcasted_iota(jnp.int32, entries.shape, 0)
    hit = (entries == wanted) & (row < live_count)
    return jnp.sum(jnp.where(hit, 1.0, 0.0), axis=0, keepdims=True)

def pattern_body(vert_rows, slash_rows, ids, lists, out_ref, taken_ref):
    vert, vcount = lists[:vert_rows], lists[vert_rows:vert_rows + 1]
    slash, scount = lists[vert_rows + 1:vert_rows + 1 + slash_rows], lists[vert_rows + 1 + slash_rows:]
    half, width = out_ref.shape[1:]
    slots = width // BLOCK
    lo = pl.multiple_of(ids[0] * half, half)
    spread = (
        lax.broadcasted_iota(jnp.int32, (slots, width), 0) == lax.broadcasted_iota(jnp.int32, (slots, width), 1) // BLOCK
    )
    spread = jnp.where(spread, 1.0, 0.0)
    for b in range(2):
        rows = []
        for slot in range(slots):
            key_block, query_block = ids[3 + slot], ids[1 + b]
            n = listed(vert, vcount, key_block) + listed(slash, scount, query_block - key_block)
            rows.append(n * jnp.where((key_block >= 0) & (key_block <= query_block), 1.0, 0.0))
        taken_ref[...] = lax.dot_general(
            jnp.concatenate(rows, axis=0), spread, (((0,), (0,)), ((), ())), preferred_element_type=jnp.float32
        )
        out_ref[b] = jnp.where(taken_ref[pl.ds(lo, half), :] > 0.5, 0.0, NEG)


def pattern_bias(ids, slots, vert_rows, slash_rows, lists):
    heads = lists.shape[1]
    vm = pl.BlockSpec(memory_space=pltpu.VMEM)
    return pl.pallas_call(
        functools.partial(pattern_body, vert_rows, slash_rows),
        out_shape=jax.ShapeDtypeStruct((2, heads // 2, slots * BLOCK), jnp.float32),
        in_specs=[pl.BlockSpec(memory_space=pltpu.SMEM), vm],
        out_specs=vm,
        scratch_shapes=[pltpu.VMEM((heads, slots * BLOCK), jnp.float32)],
        compiler_params=pltpu.CompilerParams(vmem_limit_bytes=8 * 1024 * 1024),
        cost_estimate=pl.CostEstimate(flops=0, bytes_accessed=16 << 20, transcendentals=0),
        name="pattern",
    )(ids, lists)


def stage_body(first_slot, rows_of, slots, group, scale, *refs):
    last = rows_of is not None
    (bias, q_own, q_sib), refs = refs[:3], refs[3:]
    tiles, refs = refs[:slots], refs[slots:]
    first = first_slot == 0
    keys = slice(first_slot * BLOCK, (first_slot + slots) * BLOCK)
    if not first:
        acc_in, top_in, sum_in = refs[:3]
        refs = refs[3:]
    if last:
        core, out, *refs = refs
        done_ref, *sems = refs if rows_of == "own" else (out,)
    else:
        acc_out, top_out, sum_out = refs
    kv_heads, rows, head_width = q_own.shape
    width = slots * BLOCK
    if first:
        pos = lax.broadcasted_iota(jnp.int32, (BLOCK, 1, 2 * BLOCK), 0)
        key = lax.broadcasted_iota(jnp.int32, (BLOCK, 1, 2 * BLOCK), 2)
    for b in {None: (0, 1), "own": (0,), "sibling": (1,)}[rows_of]:
        q_ref = (q_own, q_sib)[b]
        outs = []
        for g in range(kv_heads):
            k = jnp.concatenate([t[0, g] for t in tiles], axis=0)
            v = jnp.concatenate([t[1, g] for t in tiles], axis=0)
            s = lax.dot_general(q_ref[g], k, (((1,), (1,)), ((), ())), preferred_element_type=jnp.float32)
            s = s.reshape(BLOCK, group, width) + bias[b, g * group:(g + 1) * group, keys][None]
            if first:
                offset = key - b * BLOCK
                causal = jnp.where((offset > pos) & (offset < BLOCK), NEG, 0.0)
                s = jnp.concatenate([s[:, :, :2 * BLOCK] + causal, s[:, :, 2 * BLOCK:]], axis=2)
            s = s.reshape(rows, width)
            top = jnp.broadcast_to(jnp.max(s, axis=1, keepdims=True), (rows, head_width))
            if not first:
                old_top = top_in[b, g]
                top = jnp.maximum(top, old_top)
                shrink = jnp.exp2((old_top - top) * scale)
            p = jnp.exp2((s - jnp.concatenate([top] * (width // head_width), axis=1)) * scale)
            total = jnp.broadcast_to(jnp.sum(p, axis=1, keepdims=True), (rows, head_width))
            acc = jnp.dot(p.astype(jnp.bfloat16), v, preferred_element_type=jnp.float32)
            if not first:
                total = total + sum_in[b, g] * shrink
                acc = acc + acc_in[b, g] * shrink
            if not last:
                acc_out[b, g] = acc
                top_out[b, g] = top
                sum_out[b, g] = total
                continue
            outs.append((acc / total).reshape(BLOCK, group, head_width))
            if g % 2:
                pair = jnp.concatenate(outs, axis=1).astype(jnp.bfloat16)
                done_ref[:, (g - 1) * group:(g + 1) * group, :] = pair
                outs = []
    if last and rows_of == "own":
        half = kv_heads * group
        place = pl.ds(pl.multiple_of(core[0] * half, half), half)
        send = pltpu.make_async_copy(done_ref, out.at[:, place, :], sems[0])
        send.start()
        send.wait()


def attend_stage(first_slot, bias, q_own, q_sib, tiles, state, rows_of=None, core=None):
    kv_heads, rows, head_width = q_own.shape
    group = rows // BLOCK
    scale = 1.0 / math.sqrt(head_width) * math.log2(math.e)
    vm = pl.BlockSpec(memory_space=pltpu.VMEM)
    args = [bias, q_own, q_sib, *tiles, *state]
    specs, scratch = [vm] * len(args), []
    half = (BLOCK, kv_heads * group, head_width)
    if rows_of is None:
        out = [jax.ShapeDtypeStruct((2, kv_heads, rows, head_width), jnp.float32)] * 3
        out_specs = [vm] * 3
    else:
        args, specs = args + [core], specs + [pl.BlockSpec(memory_space=pltpu.SMEM)]
        out, out_specs = jax.ShapeDtypeStruct(half, jnp.bfloat16), vm
        if rows_of == "own":
            out = jax.ShapeDtypeStruct((BLOCK, 2 * half[1], head_width), jnp.bfloat16)
            out_specs = pl.BlockSpec(memory_space=pl.ANY)
            scratch = [pltpu.VMEM(half, jnp.bfloat16), pltpu.SemaphoreType.DMA]
    return pl.pallas_call(
        functools.partial(stage_body, first_slot, rows_of, len(tiles), group, scale),
        out_shape=out,
        in_specs=specs,
        out_specs=out_specs,
        scratch_shapes=scratch,
        compiler_params=pltpu.CompilerParams(vmem_limit_bytes=16 * 1024 * 1024),
        cost_estimate=pl.CostEstimate(flops=1000, bytes_accessed=1000, transcendentals=0),
        name="attend",
    )(*args)


def turn_body(core_ref, q_own, q_sib, own_ref, sib_ref):
    kv_half, rows, width = own_ref.shape
    group = rows // BLOCK
    for q_ref, out in ((q_own, own_ref), (q_sib, sib_ref)):
        for pair in range(kv_half // 2):
            lo = pl.multiple_of((core_ref[0] * kv_half + pair * 2) * group, 2 * group)
            both = q_ref[:, pl.ds(lo, 2 * group), :].astype(jnp.float32)
            for one in range(2):
                mine = both[:, one * group:(one + 1) * group, :].reshape(rows, width)
                out[pair * 2 + one] = mine.astype(jnp.bfloat16)


def turn_queries(core, own, sib, kv_total):
    positions, heads, width = own.shape
    vm = pl.BlockSpec(memory_space=pltpu.VMEM)
    half = jax.ShapeDtypeStruct((kv_total // 2, positions * heads // kv_total, width), jnp.bfloat16)
    return pl.pallas_call(
        turn_body,
        out_shape=[half, half],
        in_specs=[pl.BlockSpec(memory_space=pltpu.SMEM), vm, vm],
        out_specs=[vm, vm],
        compiler_params=pltpu.CompilerParams(vmem_limit_bytes=8 * 1024 * 1024),
        cost_estimate=pl.CostEstimate(flops=0, bytes_accessed=16 << 20, transcendentals=0),
        name="turn",
    )(core, own, sib)


def split_body(core_ref, k_hbm, v_hbm, keep_ref, give_ref, raw, turned, sems):
    half = turned.shape[1] // 2
    fetches = [pltpu.make_async_copy(hbm, raw.at[n], sems.at[n]) for n, hbm in enumerate((k_hbm, v_hbm))]
    for fetch in fetches:
        fetch.start()
    core = core_ref[0]
    for n, fetch in enumerate(fetches):
        fetch.wait()
        turned[n] = jnp.swapaxes(raw[n].astype(jnp.float32), 0, 1).astype(jnp.bfloat16)
    keep_ref[...] = turned[:, pl.ds(core * half, half)]
    give_ref[...] = turned[:, pl.ds((1 - core) * half, half)]


def split_heads(core, keys, values):
    rows, kv_total, width = keys.shape
    vm, hbm = pl.BlockSpec(memory_space=pltpu.VMEM), pl.BlockSpec(memory_space=pltpu.HBM)
    half = jax.ShapeDtypeStruct((2, kv_total // 2, rows, width), jnp.bfloat16)
    return pl.pallas_call(
        split_body,
        out_shape=[half, half],
        in_specs=[pl.BlockSpec(memory_space=pltpu.SMEM), hbm, hbm],
        out_specs=[vm, vm],
        scratch_shapes=[
            pltpu.VMEM((2, rows, kv_total, width), jnp.bfloat16),
            pltpu.VMEM((2, kv_total, rows, width), jnp.bfloat16),
            pltpu.SemaphoreType.DMA((2,)),
        ],
        compiler_params=pltpu.CompilerParams(vmem_limit_bytes=60 * 1024 * 1024),
        cost_estimate=pl.CostEstimate(flops=1000, bytes_accessed=1000, transcendentals=0),
        name="split",
    )(core, keys, values)


def join_body(core_ref, other_ref, begun_ref, out_ref, sem):
    half = other_ref.shape[1]
    place = pl.ds(pl.multiple_of((1 - core_ref[0]) * half, half), half)
    send = pltpu.make_async_copy(other_ref, out_ref.at[:, place, :], sem)
    send.start()
    send.wait()


def join_heads(core, other, begun):
    somewhere = pl.BlockSpec(memory_space=pl.ANY)
    return pl.pallas_call(
        join_body,
        out_shape=jax.ShapeDtypeStruct(begun.shape, begun.dtype),
        in_specs=[pl.BlockSpec(memory_space=pltpu.SMEM), pl.BlockSpec(memory_space=pltpu.VMEM), somewhere],
        out_specs=somewhere,
        scratch_shapes=[pltpu.SemaphoreType.DMA],
        input_output_aliases={2: 0},
        compiler_params=pltpu.CompilerParams(vmem_limit_bytes=8 * 1024 * 1024),
        cost_estimate=pl.CostEstimate(flops=1000, bytes_accessed=1000, transcendentals=0),
        name="join",
    )(core, other, begun)


def by_key_block(queries, keys, values, vert_blocks, vert_count, slash_offsets, slash_count):
    planes = lax.axis_size("seq")
    plane = lax.axis_index("seq")
    place = lax.axis_index("blk")
    core, column = place % 2, place // 2

    def trade(tile, step):
        return lax.ppermute(tile, "seq", [(i, i ^ step) for i in range(planes)])

    def across(tile):
        return lax.ppermute(tile, "blk", [(0, 2), (2, 0), (1, 3), (3, 1)])

    def sibling(tile):
        return lax.ppermute(tile, "blk", [(0, 1), (1, 0), (2, 3), (3, 2)])

    core_id = core[None]
    sibling_queries = sibling(queries)
    keep, give = split_heads(core_id, keys, values)
    slots = jnp.stack([2 * column + core, 2 * column + 1 - core, 2 * (1 - column) + core, 2 * (1 - column) + 1 - core])
    ids = jnp.concatenate(
        [jnp.stack([core, plane * 4 + slots[0], plane * 4 + slots[1]])]
        + [(plane ^ step) * 4 + slots for step in (0, 1, 3, 2)]
    )
    a, b = keep, sibling(give)
    far_a, near_a = trade(a, 3), trade(a, 1)
    late_a, b, sibling_queries = lax.optimization_barrier((a, b, sibling_queries))
    far_b, x_a, x_b = trade(b, 3), across(late_a), across(b)
    vert_lists = vert_blocks
    q_keep, q_sib = turn_queries(core_id, queries, sibling_queries, 2 * give.shape[1])
    lists = jnp.concatenate([vert_lists.T, vert_count[None], slash_offsets.T, slash_count[None]])
    bias = pattern_bias(ids, 4 * planes, vert_blocks.shape[1], slash_offsets.shape[1], lists)
    late_b, near_a, bias, q_keep, q_sib = lax.optimization_barrier((b, near_a, bias, q_keep, q_sib))
    near_b, x_near_a = trade(late_b, 1), across(near_a)
    state = attend_stage(0, bias, q_keep, q_sib, [a, b, x_a, x_b], ())
    early_a, state = lax.optimization_barrier((far_a, state))
    last_a = trade(early_a, 1)
    x_far_b = across(far_b)
    late_far_b = far_b
    last_b = trade(late_far_b, 1)
    late_far_a, x_near_a = lax.optimization_barrier((far_a, x_near_a))
    x_far_a = across(late_far_a)
    x_near_b = across(near_b)
    x_last_a, x_last_b = across(last_a), trade(x_far_b, 1)
    state = attend_stage(4, bias, q_keep, q_sib, [near_a, near_b, x_near_a, x_near_b], state)
    state = attend_stage(8, bias, q_keep, q_sib, [far_a, far_b, x_far_a, x_far_b], state)
    tiles = [last_a, last_b, x_last_a, x_last_b]
    sibling_rows = attend_stage(12, bias, q_keep, q_sib, tiles, state, "sibling", core_id)
    state, sibling_rows = lax.optimization_barrier((state, sibling_rows))
    own_rows = attend_stage(12, bias, q_keep, q_sib, tiles, state, "own", core_id)
    return join_heads(core_id, sibling(sibling_rows), own_rows)


def on_device(queries, keys, values, vert_blocks, vert_count, slash_offsets, slash_count):
    gathered = 2 * keys.size * keys.dtype.itemsize * lax.axis_size("seq") * lax.axis_size("blk")
    shape = (keys.shape[0], lax.axis_size("seq"), lax.axis_size("blk"))
    fits = gathered <= GATHER_BYTES and shape == (BLOCK, 4, 4)
    plan = by_key_block if fits else by_head_owner
    return plan(queries, keys, values, vert_blocks, vert_count, slash_offsets, slash_count)


def solution(mesh):
    return jax.shard_map(
        on_device,
        mesh=mesh,
        in_specs=(
            P(("grp", "seq", "blk"), None, None),
            P(("grp", "seq", "blk"), None, None),
            P(("grp", "seq", "blk"), None, None),
            P(),
            P(),
            P(),
            P(),
        ),
        out_specs=P(("grp", "seq", "blk"), None, None),
        check_vma=False,
    )
```

```python
import functools
import math

import jax
import jax.numpy as jnp
from jax import lax
from jax.experimental import pallas as pl
from jax.experimental.pallas import tpu as pltpu
from jax.sharding import PartitionSpec as P

BLOCK = 64
NEG = -1e30
GATHER_BYTES = 8 << 20


def slash_plan(query_index, vertical, vert_live, slash, slash_live):
    slash_index = query_index[:, None] - slash[None, :]
    duplicate = jnp.any(
        (slash_index[:, :, None] == vertical[None, None, :]) & vert_live[None, None, :], axis=2
    )
    usable = slash_live[None, :] & (slash_index >= 0) & jnp.logical_not(duplicate)
    return (slash_index, usable)


def sparse_block(
    query_tiles,
    query_index,
    vert_keys,
    vert_values,
    vertical,
    vert_live,
    slash_keys,
    slash_values,
    slash_index,
    slash_live,
):
    tile_count, block_len, head_width = query_tiles.shape
    lane_pos = jnp.arange(block_len, dtype=jnp.int32)
    query_pos = query_index[:, None] * block_len + lane_pos[None, :]
    vert_pos = vertical[:, None] * block_len + lane_pos[None, :]
    slash_pos = slash_index[:, :, None] * block_len + lane_pos[None, None, :]
    score_scale = 1.0 / math.sqrt(head_width)
    vert_scores = (
        jnp.einsum("gid,vjd->givj", query_tiles, vert_keys, preferred_element_type=jnp.float32)
        * score_scale
    )
    slash_scores = (
        jnp.einsum("gid,gsjd->gisj", query_tiles, slash_keys, preferred_element_type=jnp.float32)
        * score_scale
    )
    vert_mask = vert_live[None, None, :, None] & (
        vert_pos[None, None, :, :] <= query_pos[:, :, None, None]
    )
    slash_mask = slash_live[:, None, :, None] & (
        slash_pos[:, None, :, :] <= query_pos[:, :, None, None]
    )
    scores = jnp.concatenate(
        [
            jnp.where(vert_mask, vert_scores, -jnp.inf).reshape(tile_count, block_len, -1),
            jnp.where(slash_mask, slash_scores, -jnp.inf).reshape(tile_count, block_len, -1),
        ],
        axis=2,
    )
    row_max = jnp.max(scores, axis=2, keepdims=True)
    raised = jnp.exp(scores - row_max)
    weights = (raised / jnp.sum(raised, axis=2, keepdims=True)).astype(jnp.bfloat16)
    vert_width = vert_keys.shape[0] * block_len
    result = jnp.einsum(
        "gik,kd->gid",
        weights[:, :, :vert_width],
        vert_values.reshape(vert_width, head_width),
        preferred_element_type=jnp.float32,
    )
    result = result + jnp.einsum(
        "gik,gkd->gid",
        weights[:, :, vert_width:],
        slash_values.reshape(tile_count, -1, head_width),
        preferred_element_type=jnp.float32,
    )
    return result.astype(jnp.bfloat16).reshape(tile_count * block_len, head_width)


def by_head_owner(queries, keys, values, vert_blocks, vert_count, slash_offsets, slash_count):
    owners = lax.axis_size("seq")
    cycle_size = lax.axis_size("blk")
    owner_id = lax.axis_index("seq")
    cycle_id = lax.axis_index("blk")
    shard_rows, head_total, head_width = queries.shape
    kv_total = keys.shape[1]
    group_size = head_total // kv_total
    per_owner = head_total // owners
    kv_owned = max(1, kv_total // owners)
    sharers = max(1, owners // kv_total)
    blocks_per_shard = shard_rows // BLOCK
    query_send = queries.reshape(shard_rows, owners, per_owner, head_width)

    def by_owner(tensor):
        if sharers > 1:
            tensor = jnp.repeat(tensor, sharers, axis=1)
        return tensor.reshape(tensor.shape[0], owners, kv_owned, head_width)

    query_rows, key_part, value_part = (
        lax.all_to_all(query_send, "seq", split_axis=1, concat_axis=0, tiled=True),
        lax.all_to_all(by_owner(keys), "seq", split_axis=1, concat_axis=0, tiled=True),
        lax.all_to_all(by_owner(values), "seq", split_axis=1, concat_axis=0, tiled=True),
    )
    key_rows, value_rows = (
        lax.all_gather(key_part, "blk", axis=0, tiled=True),
        lax.all_gather(value_part, "blk", axis=0, tiled=True),
    )

    def stored(block_id):
        first_row = block_id * BLOCK
        source = first_row // shard_rows
        return (
            source % cycle_size * owners + source // cycle_size
        ) * blocks_per_shard + first_row % shard_rows // BLOCK

    key_heads = jnp.moveaxis(key_rows.reshape(-1, BLOCK, kv_owned, head_width), 2, 0)
    value_heads = jnp.moveaxis(value_rows.reshape(-1, BLOCK, kv_owned, head_width), 2, 0)
    block_total = key_heads.shape[1]
    owned_rows = owners * shard_rows
    group_rows = min(512, owned_rows)
    groups = owned_rows // group_rows
    group_blocks = group_rows // BLOCK
    query_heads = jnp.transpose(query_rows.reshape(owned_rows, per_owner, head_width), (1, 0, 2))

    def attend(step_id):
        slot_id = step_id // groups
        group_id = step_id % groups
        head_id = owner_id * per_owner + slot_id
        kv_local = head_id // group_size - owner_id // sharers * kv_owned
        head_queries = lax.dynamic_index_in_dim(query_heads, slot_id, 0, False)
        query_tiles = lax.dynamic_slice_in_dim(
            head_queries, group_id * group_rows, group_rows, 0
        ).reshape(group_blocks, BLOCK, head_width)
        local_rows = group_id * group_rows + jnp.arange(group_blocks, dtype=jnp.int32) * BLOCK
        query_index = (
            local_rows // shard_rows * cycle_size + cycle_id
        ) * blocks_per_shard + local_rows % shard_rows // BLOCK
        vertical = lax.dynamic_index_in_dim(vert_blocks, head_id, 0, False)
        vert_live = jnp.arange(vertical.shape[0], dtype=jnp.int32) < lax.dynamic_index_in_dim(
            vert_count, head_id, 0, False
        )
        slash = lax.dynamic_index_in_dim(slash_offsets, head_id, 0, False)
        slash_live = jnp.arange(slash.shape[0], dtype=jnp.int32) < lax.dynamic_index_in_dim(
            slash_count, head_id, 0, False
        )
        slash_index, usable = slash_plan(query_index, vertical, vert_live, slash, slash_live)
        clamped = stored(jnp.clip(slash_index, 0, block_total - 1))
        vert_rows = stored(vertical)
        head_keys = lax.dynamic_index_in_dim(key_heads, kv_local, 0, False)
        head_values = lax.dynamic_index_in_dim(value_heads, kv_local, 0, False)
        vert_keys = jnp.take(head_keys, vert_rows, axis=0)
        vert_values = jnp.take(head_values, vert_rows, axis=0)
        slash_keys = jnp.take(head_keys, clamped, axis=0)
        slash_values = jnp.take(head_values, clamped, axis=0)
        return sparse_block(
            query_tiles,
            query_index,
            vert_keys,
            vert_values,
            vertical,
            vert_live,
            slash_keys,
            slash_values,
            slash_index,
            usable,
        )

    attended = lax.map(attend, jnp.arange(per_owner * groups, dtype=jnp.int32))
    attended = attended.reshape(per_owner, owners, shard_rows, head_width)
    returned = lax.all_to_all(attended, "seq", split_axis=1, concat_axis=1, tiled=True)
    return jnp.transpose(returned, (2, 1, 0, 3)).reshape(shard_rows, head_total, head_width)


def listed(entries, live_count, wanted):
    row = lax.broadcasted_iota(jnp.int32, entries.shape, 0)
    hit = (entries == wanted) & (row < live_count)
    return jnp.sum(jnp.where(hit, 1.0, 0.0), axis=0, keepdims=True)

def pattern_body(vert_rows, slash_rows, ids, lists, out_ref, taken_ref):
    vert, vcount = lists[:vert_rows], lists[vert_rows:vert_rows + 1]
    slash, scount = lists[vert_rows + 1:vert_rows + 1 + slash_rows], lists[vert_rows + 1 + slash_rows:]
    half, width = out_ref.shape[1:]
    slots = width // BLOCK
    lo = pl.multiple_of(ids[0] * half, half)
    spread = (
        lax.broadcasted_iota(jnp.int32, (slots, width), 0) == lax.broadcasted_iota(jnp.int32, (slots, width), 1) // BLOCK
    )
    spread = jnp.where(spread, 1.0, 0.0)
    for b in range(2):
        rows = []
        for slot in range(slots):
            key_block, query_block = ids[3 + slot], ids[1 + b]
            n = listed(vert, vcount, key_block) + listed(slash, scount, query_block - key_block)
            rows.append(n * jnp.where((key_block >= 0) & (key_block <= query_block), 1.0, 0.0))
        taken_ref[...] = lax.dot_general(
            jnp.concatenate(rows, axis=0), spread, (((0,), (0,)), ((), ())), preferred_element_type=jnp.float32
        )
        out_ref[b] = jnp.where(taken_ref[pl.ds(lo, half), :] > 0.5, 0.0, NEG)


def pattern_bias(ids, slots, vert_rows, slash_rows, lists):
    heads = lists.shape[1]
    vm = pl.BlockSpec(memory_space=pltpu.VMEM)
    return pl.pallas_call(
        functools.partial(pattern_body, vert_rows, slash_rows),
        out_shape=jax.ShapeDtypeStruct((2, heads // 2, slots * BLOCK), jnp.float32),
        in_specs=[pl.BlockSpec(memory_space=pltpu.SMEM), vm],
        out_specs=vm,
        scratch_shapes=[pltpu.VMEM((heads, slots * BLOCK), jnp.float32)],
        compiler_params=pltpu.CompilerParams(vmem_limit_bytes=8 * 1024 * 1024),
        cost_estimate=pl.CostEstimate(flops=0, bytes_accessed=16 << 20, transcendentals=0),
        name="pattern",
    )(ids, lists)


def stage_body(first_slot, rows_of, slots, group, scale, *refs):
    last = rows_of is not None
    (bias, q_own, q_sib), refs = refs[:3], refs[3:]
    tiles, refs = refs[:slots], refs[slots:]
    first = first_slot == 0
    keys = slice(first_slot * BLOCK, (first_slot + slots) * BLOCK)
    if not first:
        acc_in, top_in, sum_in = refs[:3]
        refs = refs[3:]
    if last:
        core, out, *refs = refs
        done_ref, *sems = refs if rows_of == "own" else (out,)
    else:
        acc_out, top_out, sum_out = refs
    kv_heads, rows, head_width = q_own.shape
    width = slots * BLOCK
    sends = []
    if first:
        pos = lax.broadcasted_iota(jnp.int32, (BLOCK, 1, 2 * BLOCK), 0)
        key = lax.broadcasted_iota(jnp.int32, (BLOCK, 1, 2 * BLOCK), 2)
    for b in {None: (0, 1), "own": (0,), "sibling": (1,)}[rows_of]:
        q_ref = (q_own, q_sib)[b]
        outs = []
        for g in range(kv_heads):
            k = jnp.concatenate([t[0, g] for t in tiles], axis=0)
            v = jnp.concatenate([t[1, g] for t in tiles], axis=0)
            s = lax.dot_general(q_ref[g], k, (((1,), (1,)), ((), ())), preferred_element_type=jnp.float32)
            s = s.reshape(BLOCK, group, width) + bias[b, g * group:(g + 1) * group, keys][None]
            if first:
                offset = key - b * BLOCK
                causal = jnp.where((offset > pos) & (offset < BLOCK), NEG, 0.0)
                s = jnp.concatenate([s[:, :, :2 * BLOCK] + causal, s[:, :, 2 * BLOCK:]], axis=2)
            s = s.reshape(rows, width)
            top = jnp.broadcast_to(jnp.max(s, axis=1, keepdims=True), (rows, head_width))
            if not first:
                old_top = top_in[b, g]
                top = jnp.maximum(top, old_top)
                shrink = jnp.exp2((old_top - top) * scale)
            p = jnp.exp2((s - jnp.concatenate([top] * (width // head_width), axis=1)) * scale)
            total = jnp.broadcast_to(jnp.sum(p, axis=1, keepdims=True), (rows, head_width))
            acc = jnp.dot(p.astype(jnp.bfloat16), v, preferred_element_type=jnp.float32)
            if not first:
                total = total + sum_in[b, g] * shrink
                acc = acc + acc_in[b, g] * shrink
            if not last:
                acc_out[b, g] = acc
                top_out[b, g] = top
                sum_out[b, g] = total
                continue
            outs.append((acc / total).reshape(BLOCK, group, head_width))
            if g % 2:
                pair = jnp.concatenate(outs, axis=1).astype(jnp.bfloat16)
                part = pl.ds((g - 1) * group, 2 * group)
                done_ref[:, part, :] = pair
                outs = []
                if rows_of == "own":
                    place = pl.ds(pl.multiple_of((core[0] * kv_heads + g - 1) * group, 2 * group), 2 * group)
                    for n in range(2):
                        at = pl.ds(n * BLOCK // 2, BLOCK // 2)
                        send = pltpu.make_async_copy(done_ref.at[at, part, :], out.at[at, place, :], sems[0].at[g - 1 + n])
                        send.start()
                        sends.append(send)
    for send in sends:
        send.wait()


def attend_stage(first_slot, bias, q_own, q_sib, tiles, state, rows_of=None, core=None):
    kv_heads, rows, head_width = q_own.shape
    group = rows // BLOCK
    scale = 1.0 / math.sqrt(head_width) * math.log2(math.e)
    vm = pl.BlockSpec(memory_space=pltpu.VMEM)
    args = [bias, q_own, q_sib, *tiles, *state]
    specs, scratch = [vm] * len(args), []
    half = (BLOCK, kv_heads * group, head_width)
    if rows_of is None:
        out = [jax.ShapeDtypeStruct((2, kv_heads, rows, head_width), jnp.float32)] * 3
        out_specs = [vm] * 3
    else:
        args, specs = args + [core], specs + [pl.BlockSpec(memory_space=pltpu.SMEM)]
        out, out_specs = jax.ShapeDtypeStruct(half, jnp.bfloat16), vm
        if rows_of == "own":
            out = jax.ShapeDtypeStruct((BLOCK, 2 * half[1], head_width), jnp.bfloat16)
            out_specs = pl.BlockSpec(memory_space=pl.ANY)
            scratch = [pltpu.VMEM(half, jnp.bfloat16), pltpu.SemaphoreType.DMA((kv_heads,))]
    return pl.pallas_call(
        functools.partial(stage_body, first_slot, rows_of, len(tiles), group, scale),
        out_shape=out,
        in_specs=specs,
        out_specs=out_specs,
        scratch_shapes=scratch,
        compiler_params=pltpu.CompilerParams(vmem_limit_bytes=16 * 1024 * 1024),
        cost_estimate=pl.CostEstimate(flops=1000, bytes_accessed=1000, transcendentals=0),
        name="attend",
    )(*args)


def turn_body(core_ref, q_own, q_sib, own_ref, sib_ref):
    kv_half, rows, width = own_ref.shape
    group = rows // BLOCK
    for q_ref, out in ((q_own, own_ref), (q_sib, sib_ref)):
        for pair in range(kv_half // 2):
            lo = pl.multiple_of((core_ref[0] * kv_half + pair * 2) * group, 2 * group)
            both = q_ref[:, pl.ds(lo, 2 * group), :].astype(jnp.float32)
            for one in range(2):
                mine = both[:, one * group:(one + 1) * group, :].reshape(rows, width)
                out[pair * 2 + one] = mine.astype(jnp.bfloat16)


def turn_queries(core, own, sib, kv_total):
    positions, heads, width = own.shape
    vm = pl.BlockSpec(memory_space=pltpu.VMEM)
    half = jax.ShapeDtypeStruct((kv_total // 2, positions * heads // kv_total, width), jnp.bfloat16)
    return pl.pallas_call(
        turn_body,
        out_shape=[half, half],
        in_specs=[pl.BlockSpec(memory_space=pltpu.SMEM), vm, vm],
        out_specs=[vm, vm],
        compiler_params=pltpu.CompilerParams(vmem_limit_bytes=8 * 1024 * 1024),
        cost_estimate=pl.CostEstimate(flops=0, bytes_accessed=16 << 20, transcendentals=0),
        name="turn",
    )(core, own, sib)


def split_body(core_ref, k_hbm, v_hbm, keep_ref, give_ref, raw, turned, sems):
    half = turned.shape[1] // 2
    fetches = [pltpu.make_async_copy(hbm, raw.at[n], sems.at[n]) for n, hbm in enumerate((k_hbm, v_hbm))]
    for fetch in fetches:
        fetch.start()
    core = core_ref[0]
    for n, fetch in enumerate(fetches):
        fetch.wait()
        turned[n] = jnp.swapaxes(raw[n].astype(jnp.float32), 0, 1).astype(jnp.bfloat16)
    keep_ref[...] = turned[:, pl.ds(core * half, half)]
    give_ref[...] = turned[:, pl.ds((1 - core) * half, half)]


def split_heads(core, keys, values):
    rows, kv_total, width = keys.shape
    vm, hbm = pl.BlockSpec(memory_space=pltpu.VMEM), pl.BlockSpec(memory_space=pltpu.HBM)
    half = jax.ShapeDtypeStruct((2, kv_total // 2, rows, width), jnp.bfloat16)
    return pl.pallas_call(
        split_body,
        out_shape=[half, half],
        in_specs=[pl.BlockSpec(memory_space=pltpu.SMEM), hbm, hbm],
        out_specs=[vm, vm],
        scratch_shapes=[
            pltpu.VMEM((2, rows, kv_total, width), jnp.bfloat16),
            pltpu.VMEM((2, kv_total, rows, width), jnp.bfloat16),
            pltpu.SemaphoreType.DMA((2,)),
        ],
        compiler_params=pltpu.CompilerParams(vmem_limit_bytes=60 * 1024 * 1024),
        cost_estimate=pl.CostEstimate(flops=1000, bytes_accessed=1000, transcendentals=0),
        name="split",
    )(core, keys, values)


def join_body(core_ref, other_ref, begun_ref, out_ref, sems):
    half = other_ref.shape[1]
    place = pl.ds(pl.multiple_of((1 - core_ref[0]) * half, half), half)
    parts = sems.shape[0]
    step = other_ref.shape[0] // parts
    sends = [
        pltpu.make_async_copy(other_ref.at[pl.ds(n * step, step)], out_ref.at[pl.ds(n * step, step), place, :], sems.at[n])
        for n in range(parts)
    ]
    for send in sends:
        send.start()
    for send in sends:
        send.wait()


def join_heads(core, other, begun):
    somewhere = pl.BlockSpec(memory_space=pl.ANY)
    return pl.pallas_call(
        join_body,
        out_shape=jax.ShapeDtypeStruct(begun.shape, begun.dtype),
        in_specs=[pl.BlockSpec(memory_space=pltpu.SMEM), pl.BlockSpec(memory_space=pltpu.VMEM), somewhere],
        out_specs=somewhere,
        scratch_shapes=[pltpu.SemaphoreType.DMA((4,))],
        input_output_aliases={2: 0},
        compiler_params=pltpu.CompilerParams(vmem_limit_bytes=8 * 1024 * 1024),
        cost_estimate=pl.CostEstimate(flops=1000, bytes_accessed=1000, transcendentals=0),
        name="join",
    )(core, other, begun)


def by_key_block(queries, keys, values, vert_blocks, vert_count, slash_offsets, slash_count):
    planes = lax.axis_size("seq")
    plane = lax.axis_index("seq")
    place = lax.axis_index("blk")
    core, column = place % 2, place // 2

    def trade(tile, step):
        return lax.ppermute(tile, "seq", [(i, i ^ step) for i in range(planes)])

    def across(tile):
        return lax.ppermute(tile, "blk", [(0, 2), (2, 0), (1, 3), (3, 1)])

    def sibling(tile):
        return lax.ppermute(tile, "blk", [(0, 1), (1, 0), (2, 3), (3, 2)])

    core_id = core[None]
    sibling_queries = sibling(queries)
    keep, give = split_heads(core_id, keys, values)
    slots = jnp.stack([2 * column + core, 2 * column + 1 - core, 2 * (1 - column) + core, 2 * (1 - column) + 1 - core])
    ids = jnp.concatenate(
        [jnp.stack([core, plane * 4 + slots[0], plane * 4 + slots[1]])]
        + [(plane ^ step) * 4 + slots for step in (0, 1, 3, 2)]
    )
    a, b = keep, sibling(give)
    far_a, near_a = trade(a, 3), trade(a, 1)
    late_a, b, sibling_queries = lax.optimization_barrier((a, b, sibling_queries))
    far_b, x_a, x_b = trade(b, 3), across(late_a), across(b)
    vert_lists = vert_blocks
    q_keep, q_sib = turn_queries(core_id, queries, sibling_queries, 2 * give.shape[1])
    lists = jnp.concatenate([vert_lists.T, vert_count[None], slash_offsets.T, slash_count[None]])
    bias = pattern_bias(ids, 4 * planes, vert_blocks.shape[1], slash_offsets.shape[1], lists)
    late_b, near_a, bias, q_keep, q_sib = lax.optimization_barrier((b, near_a, bias, q_keep, q_sib))
    near_b, x_near_a = trade(late_b, 1), across(near_a)
    state = attend_stage(0, bias, q_keep, q_sib, [a, b, x_a, x_b], ())
    early_a, state = lax.optimization_barrier((far_a, state))
    last_a = trade(early_a, 1)
    x_far_b = across(far_b)
    late_far_b = far_b
    last_b = trade(late_far_b, 1)
    late_far_a, x_near_a = lax.optimization_barrier((far_a, x_near_a))
    x_far_a = across(late_far_a)
    x_near_b = across(near_b)
    x_last_a, x_last_b = across(last_a), trade(x_far_b, 1)
    state = attend_stage(4, bias, q_keep, q_sib, [near_a, near_b, x_near_a, x_near_b], state)
    state = attend_stage(8, bias, q_keep, q_sib, [far_a, far_b, x_far_a, x_far_b], state)
    tiles = [last_a, last_b, x_last_a, x_last_b]
    sibling_rows = attend_stage(12, bias, q_keep, q_sib, tiles, state, "sibling", core_id)
    state, sibling_rows = lax.optimization_barrier((state, sibling_rows))
    own_rows = attend_stage(12, bias, q_keep, q_sib, tiles, state, "own", core_id)
    return join_heads(core_id, sibling(sibling_rows), own_rows)


def on_device(queries, keys, values, vert_blocks, vert_count, slash_offsets, slash_count):
    gathered = 2 * keys.size * keys.dtype.itemsize * lax.axis_size("seq") * lax.axis_size("blk")
    shape = (keys.shape[0], lax.axis_size("seq"), lax.axis_size("blk"))
    fits = gathered <= GATHER_BYTES and shape == (BLOCK, 4, 4)
    plan = by_key_block if fits else by_head_owner
    return plan(queries, keys, values, vert_blocks, vert_count, slash_offsets, slash_count)


def solution(mesh):
    return jax.shard_map(
        on_device,
        mesh=mesh,
        in_specs=(
            P(("grp", "seq", "blk"), None, None),
            P(("grp", "seq", "blk"), None, None),
            P(("grp", "seq", "blk"), None, None),
            P(),
            P(),
            P(),
            P(),
        ),
        out_specs=P(("grp", "seq", "blk"), None, None),
        check_vma=False,
    )
```

```python
import functools
import math

import jax
import jax.numpy as jnp
from jax import lax
from jax.experimental import pallas as pl
from jax.experimental.pallas import tpu as pltpu
from jax.sharding import PartitionSpec as P

BLOCK = 64
NEG = -1e30
GATHER_BYTES = 8 << 20


def slash_plan(query_index, vertical, vert_live, slash, slash_live):
    slash_index = query_index[:, None] - slash[None, :]
    duplicate = jnp.any(
        (slash_index[:, :, None] == vertical[None, None, :]) & vert_live[None, None, :], axis=2
    )
    usable = slash_live[None, :] & (slash_index >= 0) & jnp.logical_not(duplicate)
    return (slash_index, usable)


def sparse_block(
    query_tiles,
    query_index,
    vert_keys,
    vert_values,
    vertical,
    vert_live,
    slash_keys,
    slash_values,
    slash_index,
    slash_live,
):
    tile_count, block_len, head_width = query_tiles.shape
    lane_pos = jnp.arange(block_len, dtype=jnp.int32)
    query_pos = query_index[:, None] * block_len + lane_pos[None, :]
    vert_pos = vertical[:, None] * block_len + lane_pos[None, :]
    slash_pos = slash_index[:, :, None] * block_len + lane_pos[None, None, :]
    score_scale = 1.0 / math.sqrt(head_width)
    vert_scores = (
        jnp.einsum("gid,vjd->givj", query_tiles, vert_keys, preferred_element_type=jnp.float32)
        * score_scale
    )
    slash_scores = (
        jnp.einsum("gid,gsjd->gisj", query_tiles, slash_keys, preferred_element_type=jnp.float32)
        * score_scale
    )
    vert_mask = vert_live[None, None, :, None] & (
        vert_pos[None, None, :, :] <= query_pos[:, :, None, None]
    )
    slash_mask = slash_live[:, None, :, None] & (
        slash_pos[:, None, :, :] <= query_pos[:, :, None, None]
    )
    scores = jnp.concatenate(
        [
            jnp.where(vert_mask, vert_scores, -jnp.inf).reshape(tile_count, block_len, -1),
            jnp.where(slash_mask, slash_scores, -jnp.inf).reshape(tile_count, block_len, -1),
        ],
        axis=2,
    )
    row_max = jnp.max(scores, axis=2, keepdims=True)
    raised = jnp.exp(scores - row_max)
    weights = (raised / jnp.sum(raised, axis=2, keepdims=True)).astype(jnp.bfloat16)
    vert_width = vert_keys.shape[0] * block_len
    result = jnp.einsum(
        "gik,kd->gid",
        weights[:, :, :vert_width],
        vert_values.reshape(vert_width, head_width),
        preferred_element_type=jnp.float32,
    )
    result = result + jnp.einsum(
        "gik,gkd->gid",
        weights[:, :, vert_width:],
        slash_values.reshape(tile_count, -1, head_width),
        preferred_element_type=jnp.float32,
    )
    return result.astype(jnp.bfloat16).reshape(tile_count * block_len, head_width)


def by_head_owner(queries, keys, values, vert_blocks, vert_count, slash_offsets, slash_count):
    owners = lax.axis_size("seq")
    cycle_size = lax.axis_size("blk")
    owner_id = lax.axis_index("seq")
    cycle_id = lax.axis_index("blk")
    shard_rows, head_total, head_width = queries.shape
    kv_total = keys.shape[1]
    group_size = head_total // kv_total
    per_owner = head_total // owners
    kv_owned = max(1, kv_total // owners)
    sharers = max(1, owners // kv_total)
    blocks_per_shard = shard_rows // BLOCK
    query_send = queries.reshape(shard_rows, owners, per_owner, head_width)

    def by_owner(tensor):
        if sharers > 1:
            tensor = jnp.repeat(tensor, sharers, axis=1)
        return tensor.reshape(tensor.shape[0], owners, kv_owned, head_width)

    query_rows, key_part, value_part = (
        lax.all_to_all(query_send, "seq", split_axis=1, concat_axis=0, tiled=True),
        lax.all_to_all(by_owner(keys), "seq", split_axis=1, concat_axis=0, tiled=True),
        lax.all_to_all(by_owner(values), "seq", split_axis=1, concat_axis=0, tiled=True),
    )
    key_rows, value_rows = (
        lax.all_gather(key_part, "blk", axis=0, tiled=True),
        lax.all_gather(value_part, "blk", axis=0, tiled=True),
    )

    def stored(block_id):
        first_row = block_id * BLOCK
        source = first_row // shard_rows
        return (
            source % cycle_size * owners + source // cycle_size
        ) * blocks_per_shard + first_row % shard_rows // BLOCK

    key_heads = jnp.moveaxis(key_rows.reshape(-1, BLOCK, kv_owned, head_width), 2, 0)
    value_heads = jnp.moveaxis(value_rows.reshape(-1, BLOCK, kv_owned, head_width), 2, 0)
    block_total = key_heads.shape[1]
    owned_rows = owners * shard_rows
    group_rows = min(512, owned_rows)
    groups = owned_rows // group_rows
    group_blocks = group_rows // BLOCK
    query_heads = jnp.transpose(query_rows.reshape(owned_rows, per_owner, head_width), (1, 0, 2))

    def attend(step_id):
        slot_id = step_id // groups
        group_id = step_id % groups
        head_id = owner_id * per_owner + slot_id
        kv_local = head_id // group_size - owner_id // sharers * kv_owned
        head_queries = lax.dynamic_index_in_dim(query_heads, slot_id, 0, False)
        query_tiles = lax.dynamic_slice_in_dim(
            head_queries, group_id * group_rows, group_rows, 0
        ).reshape(group_blocks, BLOCK, head_width)
        local_rows = group_id * group_rows + jnp.arange(group_blocks, dtype=jnp.int32) * BLOCK
        query_index = (
            local_rows // shard_rows * cycle_size + cycle_id
        ) * blocks_per_shard + local_rows % shard_rows // BLOCK
        vertical = lax.dynamic_index_in_dim(vert_blocks, head_id, 0, False)
        vert_live = jnp.arange(vertical.shape[0], dtype=jnp.int32) < lax.dynamic_index_in_dim(
            vert_count, head_id, 0, False
        )
        slash = lax.dynamic_index_in_dim(slash_offsets, head_id, 0, False)
        slash_live = jnp.arange(slash.shape[0], dtype=jnp.int32) < lax.dynamic_index_in_dim(
            slash_count, head_id, 0, False
        )
        slash_index, usable = slash_plan(query_index, vertical, vert_live, slash, slash_live)
        clamped = stored(jnp.clip(slash_index, 0, block_total - 1))
        vert_rows = stored(vertical)
        head_keys = lax.dynamic_index_in_dim(key_heads, kv_local, 0, False)
        head_values = lax.dynamic_index_in_dim(value_heads, kv_local, 0, False)
        vert_keys = jnp.take(head_keys, vert_rows, axis=0)
        vert_values = jnp.take(head_values, vert_rows, axis=0)
        slash_keys = jnp.take(head_keys, clamped, axis=0)
        slash_values = jnp.take(head_values, clamped, axis=0)
        return sparse_block(
            query_tiles,
            query_index,
            vert_keys,
            vert_values,
            vertical,
            vert_live,
            slash_keys,
            slash_values,
            slash_index,
            usable,
        )

    attended = lax.map(attend, jnp.arange(per_owner * groups, dtype=jnp.int32))
    attended = attended.reshape(per_owner, owners, shard_rows, head_width)
    returned = lax.all_to_all(attended, "seq", split_axis=1, concat_axis=1, tiled=True)
    return jnp.transpose(returned, (2, 1, 0, 3)).reshape(shard_rows, head_total, head_width)


def listed(entries, live_count, wanted):
    row = lax.broadcasted_iota(jnp.int32, entries.shape, 0)
    hit = (entries == wanted) & (row < live_count)
    return jnp.sum(jnp.where(hit, 1.0, 0.0), axis=0, keepdims=True)

def pattern_body(vert_rows, slash_rows, ids, lists, out_ref, taken_ref):
    vert, vcount = lists[:vert_rows], lists[vert_rows:vert_rows + 1]
    slash, scount = lists[vert_rows + 1:vert_rows + 1 + slash_rows], lists[vert_rows + 1 + slash_rows:]
    half, width = out_ref.shape[1:]
    slots = width // BLOCK
    lo = pl.multiple_of(ids[0] * half, half)
    spread = (
        lax.broadcasted_iota(jnp.int32, (slots, width), 0) == lax.broadcasted_iota(jnp.int32, (slots, width), 1) // BLOCK
    )
    spread = jnp.where(spread, 1.0, 0.0)
    for b in range(2):
        rows = []
        for slot in range(slots):
            key_block, query_block = ids[3 + slot], ids[1 + b]
            n = listed(vert, vcount, key_block) + listed(slash, scount, query_block - key_block)
            rows.append(n * jnp.where((key_block >= 0) & (key_block <= query_block), 1.0, 0.0))
        taken_ref[...] = lax.dot_general(
            jnp.concatenate(rows, axis=0), spread, (((0,), (0,)), ((), ())), preferred_element_type=jnp.float32
        )
        out_ref[b] = jnp.where(taken_ref[pl.ds(lo, half), :] > 0.5, 0.0, NEG)


def pattern_bias(ids, slots, vert_rows, slash_rows, lists):
    heads = lists.shape[1]
    vm = pl.BlockSpec(memory_space=pltpu.VMEM)
    return pl.pallas_call(
        functools.partial(pattern_body, vert_rows, slash_rows),
        out_shape=jax.ShapeDtypeStruct((2, heads // 2, slots * BLOCK), jnp.float32),
        in_specs=[pl.BlockSpec(memory_space=pltpu.SMEM), vm],
        out_specs=vm,
        scratch_shapes=[pltpu.VMEM((heads, slots * BLOCK), jnp.float32)],
        compiler_params=pltpu.CompilerParams(vmem_limit_bytes=8 * 1024 * 1024),
        cost_estimate=pl.CostEstimate(flops=0, bytes_accessed=16 << 20, transcendentals=0),
        name="pattern",
    )(ids, lists)


def stage_body(first_slot, rows_of, slots, group, scale, *refs):
    last = rows_of is not None
    (bias, q_own, q_sib), refs = refs[:3], refs[3:]
    tiles, refs = refs[:slots], refs[slots:]
    first = first_slot == 0
    keys = slice(first_slot * BLOCK, (first_slot + slots) * BLOCK)
    if not first:
        acc_in, top_in, sum_in = refs[:3]
        refs = refs[3:]
    if last:
        core, out, *refs = refs
        done_ref, *sems = refs if rows_of == "own" else (out,)
    else:
        acc_out, top_out, sum_out = refs
    kv_heads, rows, head_width = q_own.shape
    width = slots * BLOCK
    sends = []
    if first:
        pos = lax.broadcasted_iota(jnp.int32, (BLOCK, 1, 2 * BLOCK), 0)
        key = lax.broadcasted_iota(jnp.int32, (BLOCK, 1, 2 * BLOCK), 2)
    for b in {None: (0, 1), "own": (0,), "sibling": (1,)}[rows_of]:
        q_ref = (q_own, q_sib)[b]
        outs = []
        for g in range(kv_heads):
            k = jnp.concatenate([t[0, g] for t in tiles], axis=0)
            v = jnp.concatenate([t[1, g] for t in tiles], axis=0)
            s = lax.dot_general(q_ref[g], k, (((1,), (1,)), ((), ())), preferred_element_type=jnp.float32)
            s = s.reshape(BLOCK, group, width) + bias[b, g * group:(g + 1) * group, keys][None]
            if first:
                offset = key - b * BLOCK
                causal = jnp.where((offset > pos) & (offset < BLOCK), NEG, 0.0)
                s = jnp.concatenate([s[:, :, :2 * BLOCK] + causal, s[:, :, 2 * BLOCK:]], axis=2)
            s = s.reshape(rows, width)
            top = jnp.broadcast_to(jnp.max(s, axis=1, keepdims=True), (rows, head_width))
            if not first:
                old_top = top_in[b, g]
                top = jnp.maximum(top, old_top)
                shrink = jnp.exp2((old_top - top) * scale)
            p = jnp.exp2((s - jnp.concatenate([top] * (width // head_width), axis=1)) * scale)
            total = jnp.broadcast_to(jnp.sum(p, axis=1, keepdims=True), (rows, head_width))
            acc = jnp.dot(p.astype(jnp.bfloat16), v, preferred_element_type=jnp.float32)
            if not first:
                total = total + sum_in[b, g] * shrink
                acc = acc + acc_in[b, g] * shrink
            if not last:
                acc_out[b, g] = acc
                top_out[b, g] = top
                sum_out[b, g] = total
                continue
            outs.append((acc / total).reshape(BLOCK, group, head_width))
            if g % 2:
                pair = jnp.concatenate(outs, axis=1).astype(jnp.bfloat16)
                part = pl.ds((g - 1) * group, 2 * group)
                done_ref[:, part, :] = pair
                outs = []
                if rows_of == "own":
                    place = pl.ds(pl.multiple_of((core[0] * kv_heads + g - 1) * group, 2 * group), 2 * group)
                    for n in range(2):
                        at = pl.ds(n * BLOCK // 2, BLOCK // 2)
                        send = pltpu.make_async_copy(done_ref.at[at, part, :], out.at[at, place, :], sems[0].at[g - 1 + n])
                        send.start()
                        sends.append(send)
    for send in sends:
        send.wait()


def attend_stage(first_slot, bias, q_own, q_sib, tiles, state, rows_of=None, core=None):
    kv_heads, rows, head_width = q_own.shape
    group = rows // BLOCK
    scale = 1.0 / math.sqrt(head_width) * math.log2(math.e)
    vm = pl.BlockSpec(memory_space=pltpu.VMEM)
    args = [bias, q_own, q_sib, *tiles, *state]
    specs, scratch = [vm] * len(args), []
    half = (BLOCK, kv_heads * group, head_width)
    if rows_of is None:
        out = [jax.ShapeDtypeStruct((2, kv_heads, rows, head_width), jnp.float32)] * 3
        out_specs = [vm] * 3
    else:
        args, specs = args + [core], specs + [pl.BlockSpec(memory_space=pltpu.SMEM)]
        out, out_specs = jax.ShapeDtypeStruct(half, jnp.bfloat16), vm
        if rows_of == "own":
            out = jax.ShapeDtypeStruct((BLOCK, 2 * half[1], head_width), jnp.bfloat16)
            out_specs = pl.BlockSpec(memory_space=pl.ANY)
            scratch = [pltpu.VMEM(half, jnp.bfloat16), pltpu.SemaphoreType.DMA((kv_heads,))]
    return pl.pallas_call(
        functools.partial(stage_body, first_slot, rows_of, len(tiles), group, scale),
        out_shape=out,
        in_specs=specs,
        out_specs=out_specs,
        scratch_shapes=scratch,
        compiler_params=pltpu.CompilerParams(vmem_limit_bytes=16 * 1024 * 1024),
        cost_estimate=pl.CostEstimate(flops=1000, bytes_accessed=1000, transcendentals=0),
        name="attend",
    )(*args)


def turn_body(core_ref, q_own, q_sib, own_ref, sib_ref):
    kv_half, rows, width = own_ref.shape
    group = rows // BLOCK
    for q_ref, out in ((q_own, own_ref), (q_sib, sib_ref)):
        for pair in range(kv_half // 2):
            lo = pl.multiple_of((core_ref[0] * kv_half + pair * 2) * group, 2 * group)
            both = q_ref[:, pl.ds(lo, 2 * group), :].astype(jnp.float32)
            for one in range(2):
                mine = both[:, one * group:(one + 1) * group, :].reshape(rows, width)
                out[pair * 2 + one] = mine.astype(jnp.bfloat16)


def turn_queries(core, own, sib, kv_total):
    positions, heads, width = own.shape
    vm = pl.BlockSpec(memory_space=pltpu.VMEM)
    half = jax.ShapeDtypeStruct((kv_total // 2, positions * heads // kv_total, width), jnp.bfloat16)
    return pl.pallas_call(
        turn_body,
        out_shape=[half, half],
        in_specs=[pl.BlockSpec(memory_space=pltpu.SMEM), vm, vm],
        out_specs=[vm, vm],
        compiler_params=pltpu.CompilerParams(vmem_limit_bytes=8 * 1024 * 1024),
        cost_estimate=pl.CostEstimate(flops=0, bytes_accessed=16 << 20, transcendentals=0),
        name="turn",
    )(core, own, sib)


def split_body(core_ref, k_hbm, v_hbm, keep_ref, give_ref, raw, turned, sems):
    half = turned.shape[1] // 2
    fetches = [pltpu.make_async_copy(hbm, raw.at[n], sems.at[n]) for n, hbm in enumerate((k_hbm, v_hbm))]
    for fetch in fetches:
        fetch.start()
    core = core_ref[0]
    for n, fetch in enumerate(fetches):
        fetch.wait()
        turned[n] = jnp.swapaxes(raw[n].astype(jnp.float32), 0, 1).astype(jnp.bfloat16)
    keep_ref[...] = turned[:, pl.ds(core * half, half)]
    give_ref[...] = turned[:, pl.ds((1 - core) * half, half)]


def split_heads(core, keys, values):
    rows, kv_total, width = keys.shape
    vm, hbm = pl.BlockSpec(memory_space=pltpu.VMEM), pl.BlockSpec(memory_space=pltpu.HBM)
    half = jax.ShapeDtypeStruct((2, kv_total // 2, rows, width), jnp.bfloat16)
    return pl.pallas_call(
        split_body,
        out_shape=[half, half],
        in_specs=[pl.BlockSpec(memory_space=pltpu.SMEM), hbm, hbm],
        out_specs=[vm, vm],
        scratch_shapes=[
            pltpu.VMEM((2, rows, kv_total, width), jnp.bfloat16),
            pltpu.VMEM((2, kv_total, rows, width), jnp.bfloat16),
            pltpu.SemaphoreType.DMA((2,)),
        ],
        compiler_params=pltpu.CompilerParams(vmem_limit_bytes=60 * 1024 * 1024),
        cost_estimate=pl.CostEstimate(flops=1000, bytes_accessed=1000, transcendentals=0),
        name="split",
    )(core, keys, values)


def join_body(core_ref, other_ref, begun_ref, out_ref, sems):
    half = other_ref.shape[1]
    place = pl.ds(pl.multiple_of((1 - core_ref[0]) * half, half), half)
    parts = sems.shape[0]
    step = other_ref.shape[0] // parts
    sends = [
        pltpu.make_async_copy(other_ref.at[pl.ds(n * step, step)], out_ref.at[pl.ds(n * step, step), place, :], sems.at[n])
        for n in range(parts)
    ]
    for send in sends:
        send.start()
    for send in sends:
        send.wait()


def join_heads(core, other, begun):
    somewhere = pl.BlockSpec(memory_space=pl.ANY)
    return pl.pallas_call(
        join_body,
        out_shape=jax.ShapeDtypeStruct(begun.shape, begun.dtype),
        in_specs=[pl.BlockSpec(memory_space=pltpu.SMEM), pl.BlockSpec(memory_space=pltpu.VMEM), somewhere],
        out_specs=somewhere,
        scratch_shapes=[pltpu.SemaphoreType.DMA((4,))],
        input_output_aliases={2: 0},
        compiler_params=pltpu.CompilerParams(vmem_limit_bytes=8 * 1024 * 1024),
        cost_estimate=pl.CostEstimate(flops=1000, bytes_accessed=1000, transcendentals=0),
        name="join",
    )(core, other, begun)


def by_key_block(queries, keys, values, vert_blocks, vert_count, slash_offsets, slash_count):
    planes = lax.axis_size("seq")
    plane = lax.axis_index("seq")
    place = lax.axis_index("blk")
    core, column = place % 2, place // 2

    def trade(tile, step):
        return lax.ppermute(tile, "seq", [(i, i ^ step) for i in range(planes)])

    def across(tile):
        return lax.ppermute(tile, "blk", [(0, 2), (2, 0), (1, 3), (3, 1)])

    def sibling(tile):
        return lax.ppermute(tile, "blk", [(0, 1), (1, 0), (2, 3), (3, 2)])

    core_id = core[None]
    sibling_queries = sibling(queries)
    keep, give = split_heads(core_id, keys, values)
    slots = jnp.stack([2 * column + core, 2 * column + 1 - core, 2 * (1 - column) + core, 2 * (1 - column) + 1 - core])
    ids = jnp.concatenate(
        [jnp.stack([core, plane * 4 + slots[0], plane * 4 + slots[1]])]
        + [(plane ^ step) * 4 + slots for step in (0, 1, 3, 2)]
    )
    a, b = keep, sibling(give)
    far_a, near_a = trade(a, 3), trade(a, 1)
    late_a, b, sibling_queries = lax.optimization_barrier((a, b, sibling_queries))
    far_b, x_a, x_b = trade(b, 3), across(late_a), across(b)
    vert_lists = vert_blocks
    q_keep, q_sib = turn_queries(core_id, queries, sibling_queries, 2 * give.shape[1])
    lists = jnp.concatenate([vert_lists.T, vert_count[None], slash_offsets.T, slash_count[None]])
    bias = pattern_bias(ids, 4 * planes, vert_blocks.shape[1], slash_offsets.shape[1], lists)
    late_b, near_a, bias, x_b = lax.optimization_barrier((b, near_a, bias, x_b))
    near_b, x_near_a = trade(late_b, 1), across(near_a)
    state = attend_stage(0, bias, q_keep, q_sib, [a, b, x_a, x_b], ())
    early_a, state = lax.optimization_barrier((far_a, state))
    last_a = trade(early_a, 1)
    x_far_b = across(far_b)
    late_far_b = far_b
    last_b = trade(late_far_b, 1)
    late_far_a, x_near_a = lax.optimization_barrier((far_a, x_near_a))
    x_far_a = across(late_far_a)
    x_near_b = across(near_b)
    x_last_a, x_last_b = across(last_a), trade(x_far_b, 1)
    state = attend_stage(4, bias, q_keep, q_sib, [near_a, near_b, x_near_a, x_near_b], state)
    state = attend_stage(8, bias, q_keep, q_sib, [far_a, far_b, x_far_a, x_far_b], state)
    tiles = [last_a, last_b, x_last_a, x_last_b]
    sibling_rows = attend_stage(12, bias, q_keep, q_sib, tiles, state, "sibling", core_id)
    state, sibling_rows = lax.optimization_barrier((state, sibling_rows))
    own_rows = attend_stage(12, bias, q_keep, q_sib, tiles, state, "own", core_id)
    return join_heads(core_id, sibling(sibling_rows), own_rows)


def on_device(queries, keys, values, vert_blocks, vert_count, slash_offsets, slash_count):
    gathered = 2 * keys.size * keys.dtype.itemsize * lax.axis_size("seq") * lax.axis_size("blk")
    shape = (keys.shape[0], lax.axis_size("seq"), lax.axis_size("blk"))
    fits = gathered <= GATHER_BYTES and shape == (BLOCK, 4, 4)
    plan = by_key_block if fits else by_head_owner
    return plan(queries, keys, values, vert_blocks, vert_count, slash_offsets, slash_count)


def solution(mesh):
    return jax.shard_map(
        on_device,
        mesh=mesh,
        in_specs=(
            P(("grp", "seq", "blk"), None, None),
            P(("grp", "seq", "blk"), None, None),
            P(("grp", "seq", "blk"), None, None),
            P(),
            P(),
            P(),
            P(),
        ),
        out_specs=P(("grp", "seq", "blk"), None, None),
        check_vma=False,
    )
```
